128 devices in a mesh: dp: 16 (over z, x), enc: 8 (over y, core).
Axes of the slice: x: 4, y: 4, z: 4, core: 2. Of those that a mesh axis runs over, the one named last changes fastest.
Arguments:
- chars: int32 [786432, 50], P('dp'), may hold values from 0 to 261
- char_table: bfloat16 [262, 16], replicated, may hold values from -6 to 6
- conv_weight: bfloat16 [7, 16, 2048], P(None, None, 'enc'), may hold values from -0.75 to 0.75
- conv_bias: float32 [2048], P('enc'), may hold values from -3 to 3
- hw_weight: bfloat16 [2, 2048, 2, 2048], P(None, None, None, 'enc'), may hold values from -0.125 to 0.125
- hw_bias: float32 [2, 2, 2048], P(None, None, 'enc'), may hold values from -4 to 4
- proj_weight: bfloat16 [2048, 512], P('enc'), may hold values from -0.125 to 0.125
- proj_bias: float32 [512], P('enc'), may hold values from -3 to 3
- owner_types: int32 [16384], P('dp'), may hold values from 0 to 49151, as said below
- requests: int32 [16, 16, 256], P('dp'), may hold values from -1 to 1023, as said below
- tok_slot: int32 [131072], P('dp'), may hold values from 0 to 4095, as said below
- d_tokens: bfloat16 [131072, 512], P('dp', 'enc'), may hold values from -0.59765625 to 0.59765625
Outputs:
- token_vectors: bfloat16 [131072, 512], P('dp', 'enc')
- d_features: bfloat16 [16384, 2048], P('dp', 'enc')
- d_highway: float32 [2, 2048, 2, 2048], P(None, 'dp', None, 'enc')
- d_projection: float32 [2048, 512], P('enc', 'dp')
The draws below stay inside these ranges and needn't reach their ends.
Inputs may be any that keep to these rules, and one draw needn't show every extreme that they name: `owner_types`: entries o * 1024 to (o + 1) * 1024 - 1 are distinct rows of owner o's 49152 rows of chars; every owner's list holds its first and its last row. `requests`: list (r, o) holds 64 to 256 distinct positions of owner o's unique list, then -1 entries. Every position of every owner's list is asked for by some replica. In every draw one owner receives full lists (256 positions) from every replica, and some list is not full. `tok_slot`: token t of replica r names a slot o * 256 + k with requests[r, o, k] >= 0; every such slot is named by at least one token of replica r.
All inputs are finite; a program needn't handle non-finite values.
Results may differ from the reference program's by a relative error of at most 0.015.
Values may be sent and summed in bfloat16 or wider, within the bound.
A program may use at most 192 MiB of HBM per device.

```python
import math
import jax
import jax.numpy as jnp
from jax import lax

F = 2048
P_SIZE = 512
CE = 16
CH = 50
NCHAR = 262
TAPS = 7
HW_LAYERS = 2
TYPES_DEV = 49152
UNIQ = 1024
CAP = 256
TOK_REP = 8192
TYPES = 786432
TOKENS = 131072
N_DP = 16
N_ENC = 8


def request_plan(key):
    base = jax.random.fold_in(key, 4242)
    keys = jax.random.split(base, 8)
    owners = 4 * UNIQ // CAP
    quarter = CAP // 4
    level = jax.random.randint(keys[0], (owners,), 1, 5)
    cutback = jax.random.randint(keys[1], (owners, owners), 0, CAP // 8 + 1)
    counts = jnp.maximum(level[None, :] * quarter - cutback, quarter)
    full_owner = jax.random.randint(keys[2], (), 0, owners)
    lucky = jax.random.randint(keys[3], (), 0, owners)
    columns = jnp.arange(owners)
    replicas = jnp.arange(owners)
    counts = jnp.where(columns[None, :] == full_owner, CAP, counts)
    light = (replicas[:, None] == (lucky + 1) % owners) & (columns[None, :] == (full_owner + 1) % owners)
    counts = jnp.where(light, quarter, counts)
    heavy = (replicas[:, None] == lucky) & (columns[None, :] == owners - 1)
    counts = jnp.where(heavy, CAP, counts)
    list_keys = jax.random.split(keys[4], owners * owners)
    shuffles = jax.vmap(lambda one_key: jax.random.permutation(one_key, UNIQ))(list_keys)
    shuffles = shuffles.reshape(owners, owners, UNIQ).astype(jnp.int32)
    position = jnp.arange(UNIQ, dtype=jnp.int32)
    others = (position[None, None, :] % owners != replicas[:, None, None]).astype(jnp.int32)
    scores = others * 2 ** 22 + shuffles
    picks = jnp.argsort(scores, axis=2, stable=True)[:, :, :CAP].astype(jnp.int32)
    live = jnp.arange(CAP)[None, None, :] < counts[:, :, None]
    requests = jnp.where(live, picks, -1).astype(jnp.int32)
    slots = owners * CAP
    live_flat = live.reshape(owners, slots).astype(jnp.int32)
    slot_keys = jax.random.split(keys[5], owners)
    slot_shuffle = jax.vmap(lambda one_key: jax.random.permutation(one_key, slots))(slot_keys).astype(jnp.int32)
    order = jnp.argsort((1 - live_flat) * 2 ** 22 + slot_shuffle, axis=1, stable=True).astype(jnp.int32)
    live_total = jnp.sum(live_flat, axis=1)
    draws = jax.random.randint(keys[6], (owners, TOK_REP), 0, 2 ** 20) % live_total[:, None]
    token_index = jnp.arange(TOK_REP, dtype=jnp.int32)[None, :]
    chosen = jnp.where(token_index < live_total[:, None], token_index, draws * draws // live_total[:, None])
    token_slots = jnp.take_along_axis(order, chosen, axis=1)
    token_keys = jax.random.split(keys[7], owners)
    token_shuffle = jax.vmap(lambda one_key: jax.random.permutation(one_key, TOK_REP))(token_keys).astype(jnp.int32)
    token_slots = jnp.take_along_axis(token_slots, token_shuffle, axis=1)
    return (requests, token_slots.reshape(-1).astype(jnp.int32))


def draw_requests(key, part):
    return request_plan(key)[0]


def draw_tok_slot(key, part):
    return request_plan(key)[1]


def owner_list(one_key):
    first_key, second_key = jax.random.split(one_key)
    inner = jax.random.permutation(first_key, TYPES_DEV - 2)[:UNIQ - 2].astype(jnp.int32) + 1
    ends = jnp.array([0, TYPES_DEV - 1], dtype=jnp.int32)
    listed = jnp.concatenate([ends, inner])
    order = jax.random.permutation(second_key, UNIQ)
    return listed[order]


def draw_owner_types(key, part):
    owners = 4 * UNIQ // CAP
    type_keys = jax.random.split(jax.random.fold_in(key, 77), owners)
    chosen = jax.vmap(owner_list)(type_keys)
    return chosen.reshape(-1).astype(jnp.int32)


def set_ends(values, own_key, smallest, high):
    dims = values.shape
    index_at = [jax.random.randint(jax.random.fold_in(own_key, axis), (), 0, dims[axis]) for axis in range(len(dims))]
    values = values.at[tuple(index_at)].set(smallest)
    longest = dims.index(max(dims))
    index_at[longest] = (index_at[longest] + 1) % dims[longest]
    return values.at[tuple(index_at)].set(high)


def steps_of(key, extent, cuts, least, high):
    level, own = 1.0, jax.random.fold_in(key, 6)
    for dim, shards_of in cuts:
        heights = jnp.exp(jax.random.uniform(jax.random.fold_in(own, dim), (shards_of,), jnp.float32, least / len(cuts), high / len(cuts)))
        level = level * jnp.repeat(heights, extent[dim] // shards_of).reshape([-1 if axis == dim else 1 for axis in range(len(extent))])
    return level


def gaussian(rng, extent, spread, limit, cuts=(), held_as=jnp.bfloat16):
    entries = spread * jax.random.normal(rng, extent, jnp.float32)
    if cuts:
        entries = entries * steps_of(rng, extent, cuts, -0.22, 0.18)
    return jnp.clip(entries, -limit, limit).astype(held_as)


def setup_inputs(seed: int = 0) -> dict:
    key_of = jax.random.split(jax.random.key(seed), 13)
    return {
        "chars": set_ends(jax.random.randint(key_of[0], (TYPES, CH), 0, NCHAR), jax.random.fold_in(key_of[0], 1), 0, NCHAR - 1).astype(jnp.int32),
        "char_table": gaussian(key_of[1], (NCHAR, CE), 1.0, 6.0),
        "conv_weight": gaussian(key_of[2], (TAPS, CE, F), (4 * CE) ** -0.5, 0.75, ((2, 8),)),
        "conv_bias": gaussian(key_of[3], (F,), 0.5, 3.0, ((0, 8),), jnp.float32),
        "hw_weight": gaussian(key_of[4], (HW_LAYERS, F, 2, F), F ** -0.5, 0.125, ((3, 8),)),
        "hw_bias": gaussian(key_of[5], (HW_LAYERS, 2, F), 1.0, 4.0, ((2, 8),), jnp.float32),
        "proj_weight": gaussian(key_of[6], (F, P_SIZE), F ** -0.5, 0.125, ((0, 8),)),
        "proj_bias": gaussian(key_of[7], (P_SIZE,), 0.5, 3.0, ((0, 8),), jnp.float32),
        "owner_types": draw_owner_types(jax.random.fold_in(key_of[12], 71), 0),
        "requests": draw_requests(jax.random.fold_in(key_of[12], 71), 0),
        "tok_slot": draw_tok_slot(jax.random.fold_in(key_of[12], 71), 0),
        "d_tokens": gaussian(key_of[11], (TOKENS, P_SIZE), 0.1, 0.59765625, ((0, 16), (1, 8))),
    }


def filter_widths(total_filters):
    filter_index = jnp.arange(total_filters, dtype=jnp.int32)
    width = jnp.ones((total_filters,), jnp.int32)
    for share in (1, 2, 4, 8, 16, 32):
        width = width + (filter_index >= share * total_filters // 64).astype(jnp.int32)
    return width


def encode_words(word_chars, char_table, conv_weight, conv_bias):
    taps, embed_width, total_filters = conv_weight.shape
    length = word_chars.shape[1]
    width = filter_widths(total_filters)
    tap_mask = jnp.arange(taps, dtype=jnp.int32)[:, None] < width[None, :]
    kernel = jnp.where(tap_mask[:, None, :], conv_weight, jnp.zeros_like(conv_weight))
    kernel = kernel.reshape(taps * embed_width, total_filters).astype(jnp.float32)
    valid = jnp.arange(length, dtype=jnp.int32)[:, None] + width[None, :] <= length

    def encode_block(block_chars):
        vectors = char_table[block_chars]
        shifted = jnp.pad(vectors, ((0, 0), (0, taps - 1), (0, 0)))
        windows = jnp.concatenate([shifted[:, tap:tap + length, :] for tap in range(taps)], axis=2)
        conv = jnp.einsum('bpk,kf->bpf', windows.astype(jnp.float32), kernel)
        conv = jnp.where(valid[None], conv, -jnp.inf)
        return jnp.maximum(jnp.max(conv, axis=1) + conv_bias, 0.0).astype(jnp.bfloat16)

    rows = word_chars.shape[0]
    block = math.gcd(rows, 128)
    pooled = lax.map(encode_block, word_chars.reshape(rows // block, block, length))
    return pooled.reshape(rows, total_filters)


def reference(chars, char_table, conv_weight, conv_bias, hw_weight, hw_bias, proj_weight, proj_bias, owner_types, requests, tok_slot, d_tokens):
    layers = hw_weight.shape[0]
    total_filters = hw_weight.shape[1]
    owners = N_DP
    owner_base = (jnp.arange(owners, dtype=jnp.int32) * TYPES_DEV)[:, None]
    global_types = (owner_types.reshape(owners, UNIQ) + owner_base).reshape(-1)
    word_chars = chars[global_types]
    features = encode_words(word_chars, char_table, conv_weight, conv_bias)
    rows = features.shape[0]

    layer_input = features
    saved = []
    for layer in range(layers):
        weight_rows = hw_weight[layer].reshape(total_filters, 2 * total_filters)
        pre = jnp.dot(layer_input, weight_rows, preferred_element_type=jnp.float32)
        transform = pre[:, :total_filters] + hw_bias[layer, 0]
        gate = jax.nn.sigmoid(pre[:, total_filters:] + hw_bias[layer, 1])
        saved.append((layer_input, transform, gate))
        mixed = gate * jax.nn.silu(transform) + (1.0 - gate) * layer_input.astype(jnp.float32)
        layer_input = mixed.astype(jnp.bfloat16)
    top = layer_input
    encoded = (jnp.dot(top, proj_weight, preferred_element_type=jnp.float32) + proj_bias).astype(jnp.bfloat16)

    slots = owners * CAP
    owner_rows = jnp.arange(owners, dtype=jnp.int32)[None, :, None] * UNIQ
    slot_rows = (owner_rows + jnp.maximum(requests, 0)).reshape(owners, slots)
    token_slots = tok_slot.reshape(owners, TOK_REP)
    token_rows = jnp.take_along_axis(slot_rows, token_slots, axis=1).reshape(-1)
    token_vectors = encoded[token_rows]

    segment_index = (jnp.arange(owners, dtype=jnp.int32)[:, None] * slots + token_slots).reshape(-1)
    slot_grads = jax.ops.segment_sum(d_tokens.astype(jnp.float32), segment_index, num_segments=owners * slots)
    slot_grads = slot_grads.astype(jnp.bfloat16)
    targets = jnp.where(requests >= 0, owner_rows + requests, rows).reshape(-1)
    row_grads = jax.ops.segment_sum(slot_grads.astype(jnp.float32), targets, num_segments=rows + 1)[:rows]
    row_grads = row_grads.astype(jnp.bfloat16)

    d_projection = jnp.dot(top.T, row_grads, preferred_element_type=jnp.float32)
    upstream = jnp.dot(row_grads, proj_weight.T, preferred_element_type=jnp.float32)
    group = total_filters // N_ENC
    grads = [None] * layers
    for layer in reversed(range(layers)):
        layer_in, transform, gate = saved[layer]
        weight = hw_weight[layer]
        sigma = jax.nn.sigmoid(transform)
        activated = transform * sigma
        slope = sigma * (1.0 + transform * (1.0 - sigma))
        transform_grad = upstream * gate * slope
        gate_grad = upstream * (activated - layer_in.astype(jnp.float32)) * gate * (1.0 - gate)
        pre_grads = jnp.stack([transform_grad, gate_grad], axis=1).astype(jnp.bfloat16)
        whole_grads = jnp.dot(layer_in.T, pre_grads.reshape(rows, 2 * total_filters), preferred_element_type=jnp.float32)
        grads[layer] = whole_grads.reshape(total_filters, 2, total_filters)
        back = upstream * (1.0 - gate)
        for part in range(N_ENC):
            grads_part = pre_grads[:, :, part * group:(part + 1) * group].reshape(rows, 2 * group)
            weight_part = weight[:, :, part * group:(part + 1) * group].reshape(total_filters, 2 * group)
            term = lax.dot_general(grads_part, weight_part, (((1,), (1,)), ((), ())), preferred_element_type=jnp.float32)
            back = back + lax.optimization_barrier(term.astype(jnp.bfloat16)).astype(jnp.float32)
        upstream = back
    d_features = upstream.astype(jnp.bfloat16)
    return token_vectors, d_features, jnp.stack(grads), d_projection
```

```python
import functools
import jax
import jax.numpy as jnp
from jax import lax
from jax.experimental import pallas as pl
from jax.experimental.pallas import tpu as pltpu
from jax.sharding import PartitionSpec as P

BF = jnp.bfloat16
F32 = jnp.float32
VM = pl.BlockSpec(memory_space=pltpu.VMEM)
BASE = 128


def width_of(index, total):
    width = jnp.ones(index.shape, jnp.int32)
    for share in (1, 2, 4, 8, 16, 32):
        width = width + (index >= share * total // 64).astype(jnp.int32)
    return width


def one_hot(row, count):
    n = row.shape[1]
    return jnp.where(
        lax.broadcasted_iota(jnp.int32, (count, n), 0) == row, 1.0, 0.0
    ).astype(BF)


def nt(a, b):
    return lax.dot_general(a, b, (((1,), (1,)), ((), ())), preferred_element_type=F32)


def nn(a, b):
    return jnp.dot(a, b, preferred_element_type=F32)


def tn(a, b):
    return lax.dot_general(a, b, (((0,), (0,)), ((), ())), preferred_element_type=F32)


def column(row):
    return jnp.broadcast_to(row, (128, row.shape[1])).T[:, :1]


def encode_kernel(total, length, chars_ref, types_ref, table_ref, weight_ref, bias_ref,
                  out_ref, hot, lhs, acc, vec, band, best):
    step = pl.program_id(0)
    words = types_ref.shape[1]
    lanes = 256
    group = chars_ref.shape[1] // lanes
    rows = 64

    @pl.when(step == 0)
    def _():
        hot[...] = one_hot(types_ref[...] & (lanes - 1), lanes)
        acc[...] = jnp.zeros_like(acc)
        lhs[...] = jnp.zeros_like(lhs)

    high = types_ref[...] // lanes
    for part in range(group // 8):
        for j in range(8):
            block = chars_ref[:, (part * 8 + j) * lanes:(part * 8 + j + 1) * lanes]
            lhs[j * rows:j * rows + length, :] = (block - BASE).astype(F32).astype(BF)
        for half in range(words // 256):
            cols = slice(half * 256, half * 256 + 256)
            picked = nn(lhs[...], hot[:, cols])
            here = acc[:, cols]
            for j in range(8):
                here = jnp.where(high[:, cols] == step * group + part * 8 + j,
                                 picked[j * rows:(j + 1) * rows], here)
            acc[:, cols] = here

    @pl.when(step == pl.num_programs(0) - 1)
    def _():
        filters = weight_ref.shape[1]
        vec[length * 16:, :] = jnp.zeros((vec.shape[0] - length * 16, words), BF)

        def embed(p, carry):
            row = acc[pl.ds(p, 1), :].astype(jnp.int32) + BASE
            for b in range(words // 128):
                idx = jnp.broadcast_to(row[:, b * 128:(b + 1) * 128], (8, 128))
                low, seg = idx & 127, idx >> 7
                halves = []
                for h in range(2):
                    got = None
                    for s in range(3):
                        tab = table_ref[h * 8:(h + 1) * 8, s * 128:(s + 1) * 128]
                        val = jnp.take_along_axis(tab, low, axis=1)
                        got = val if got is None else jnp.where(seg == s, val, got)
                    halves.append(got)
                vec[pl.ds(pl.multiple_of(p * 16, 16), 16), b * 128:(b + 1) * 128] = (
                    jnp.concatenate(halves, axis=0).astype(BF))
            return carry

        lax.fori_loop(0, length, embed, 0)

        base = lax.axis_index("enc") * filters
        width_row = width_of(base + lax.broadcasted_iota(jnp.int32, (128, filters), 1), total)
        tap = lax.broadcasted_iota(jnp.int32, (128, filters), 0) // 16
        raw = jnp.concatenate(
            [weight_ref[...].astype(F32), jnp.zeros((128 - weight_ref.shape[0], filters), F32)],
            axis=0)
        kt = jnp.where(tap < width_row, raw, 0.0).T
        wide = jnp.concatenate([kt, jnp.zeros((filters, 128), F32)], axis=1)
        for q in range(8):
            moved = wide if q == 0 else pltpu.roll(wide, q * 16, 1)
            band[q * filters:(q + 1) * filters, :] = moved.astype(BF)
        best[...] = jnp.full(best.shape, -jnp.inf, F32)
        width_col = width_of(base + lax.broadcasted_iota(jnp.int32, (filters, 256), 0), total)
        groups = -(-length // 8)

        def conv(g, first, count, masked):
            for half in range(words // 256):
                cols = slice(half * 256, half * 256 + 256)
                win = vec[pl.ds(pl.multiple_of(g * 128, 128), 256), cols]
                out = nn(band[:count * filters, :], win)
                m = best[:, cols]
                for q in range(count):
                    val = out[q * filters:(q + 1) * filters]
                    if masked and first + q + 7 > length:
                        val = jnp.where(width_col <= length - first - q, val, -jnp.inf)
                    m = jnp.maximum(m, val)
                best[:, cols] = m

        def body(g, carry):
            conv(g, 0, 8, False)
            return carry

        lax.fori_loop(0, groups - 2, body, 0)
        for g in (groups - 2, groups - 1):
            conv(g, g * 8, min(8, length - g * 8), True)
        out_ref[...] = jnp.maximum(best[...] + column(bias_ref[...]), 0.0).astype(BF)


def encode(chars_t, types, table_t, weight, bias, total):
    length, count = chars_t.shape
    words = types.shape[1]
    filters = weight.shape[1]
    block = 4096
    return pl.pallas_call(
        functools.partial(encode_kernel, total, length),
        grid=(count // block,),
        in_specs=[pl.BlockSpec((length, block), lambda i: (0, i)), VM, VM, VM, VM],
        out_specs=VM,
        out_shape=jax.ShapeDtypeStruct((filters, words), BF),
        scratch_shapes=[
            pltpu.VMEM((256, words), BF),
            pltpu.VMEM((512, 256), BF),
            pltpu.VMEM((64, words), F32),
            pltpu.VMEM((1024, words), BF),
            pltpu.VMEM((8 * filters, 256), BF),
            pltpu.VMEM((filters, words), F32),
        ],
        compiler_params=pltpu.CompilerParams(vmem_limit_bytes=48 << 20),
    )(chars_t, types, table_t, weight, bias)


def slot_sums(slot_ref, d_ref, out_ref, acc, chunk=1024):
    c, tokens = d_ref.shape
    owners = out_ref.shape[0] // c
    acc[...] = jnp.zeros_like(acc)

    def body(i, carry):
        at = pl.ds(pl.multiple_of(i * chunk, chunk), chunk)
        slot = slot_ref[:, at]
        hot = one_hot(slot & 255, 256)
        high = slot >> 8
        d = d_ref[:, at]
        parts = [d * jnp.where(high == o, 1.0, 0.0).astype(BF) for o in range(owners)]
        acc[...] += nt(jnp.concatenate(parts, axis=0), hot)
        return carry

    lax.fori_loop(0, tokens // chunk, body, 0)
    out_ref[...] = acc[...].astype(BF)


def token_pick(slot_ref, ret_ref, out_ref, chunk=1024):
    c, tokens = out_ref.shape
    owners = ret_ref.shape[0] // c

    def body(i, carry):
        at = pl.ds(pl.multiple_of(i * chunk, chunk), chunk)
        slot = slot_ref[:, at]
        got = nn(ret_ref[...], one_hot(slot & 255, 256))
        high = slot >> 8
        out = jnp.zeros((c, chunk), F32)
        for o in range(owners):
            out = jnp.where(high == o, got[o * c:(o + 1) * c], out)
        out_ref[:, at] = out.astype(BF)
        return carry

    lax.fori_loop(0, tokens // chunk, body, 0)


def owner_sums(asked_ref, arr_ref, out_ref):
    c, unique = out_ref.shape
    reps, cap = asked_ref.shape
    acc = jnp.zeros((unique // 256 * c, 256), F32)
    for r in range(reps):
        asked = asked_ref[r:r + 1, :]
        hot = one_hot(asked & 255, 256)
        a = arr_ref[r * c:(r + 1) * c, :]
        parts = [a * jnp.where((asked >> 8) == h, 1.0, 0.0).astype(BF) for h in range(unique // 256)]
        acc += nt(jnp.concatenate(parts, axis=0), hot)
    for h in range(unique // 256):
        out_ref[:, h * 256:(h + 1) * 256] = acc[h * c:(h + 1) * c].astype(BF)


def owner_pick(asked_ref, enc_ref, out_ref):
    c, unique = enc_ref.shape
    reps, cap = asked_ref.shape
    enc = enc_ref[...]
    tall = jnp.concatenate([enc[:, h * 256:(h + 1) * 256] for h in range(unique // 256)], axis=0)
    for r in range(reps):
        asked = asked_ref[r:r + 1, :]
        got = nn(tall, one_hot(asked & 255, 256))
        out = jnp.zeros((c, cap), F32)
        for h in range(unique // 256):
            out = jnp.where((asked >> 8) == h, got[h * c:(h + 1) * c], out)
        out_ref[r * c:(r + 1) * c, :] = out.astype(BF)


def local(body, shape, scratch, *args):
    return pl.pallas_call(
        body, in_specs=[VM] * len(args), out_specs=VM,
        out_shape=jax.ShapeDtypeStruct(shape, BF), scratch_shapes=scratch,
        compiler_params=pltpu.CompilerParams(vmem_limit_bytes=48 << 20),
    )(*args)


def per_device(chars, char_table, conv_weight, conv_bias, hw_weight, hw_bias, proj_weight,
               proj_bias, owner_types, requests, tok_slot, d_tokens):
    taps, embed_width, filters = conv_weight.shape
    layers, total = hw_weight.shape[:2]
    unique = owner_types.shape[0]
    owners, cap = requests.shape[1:]
    tokens, c = d_tokens.shape
    table_t = jnp.pad(char_table.T.astype(F32), ((0, 0), (0, 384 - char_table.shape[0])))
    features = encode(chars.T, owner_types.reshape(1, unique), table_t,
                      conv_weight.reshape(taps * embed_width, filters),
                      conv_bias.reshape(1, filters), total)
    slot = tok_slot.reshape(1, tokens)
    asked = lax.all_to_all(requests[0], "dp", split_axis=0, concat_axis=0, tiled=True)
    slot_grads = local(slot_sums, (owners * c, cap), [pltpu.VMEM((owners * c, cap), F32)],
                       slot, d_tokens.T)
    arrived = lax.all_to_all(slot_grads, "dp", split_axis=0, concat_axis=0, tiled=True)
    row_grads = local(owner_sums, (c, unique), [], asked, arrived)
    full_grads = lax.all_gather(row_grads, "enc", axis=0, tiled=True)

    layer_input = features
    saved = []
    for layer in range(layers):
        rows = hw_weight[layer].reshape(total, 2 * filters)
        whole = lax.all_gather(layer_input, "enc", axis=0, tiled=True)
        pre = tn(rows, whole)
        transform = pre[:filters] + hw_bias[layer, 0][:, None]
        gate = jax.nn.sigmoid(pre[filters:] + hw_bias[layer, 1][:, None])
        saved.append((layer_input, whole, transform, gate))
        mixed = gate * jax.nn.silu(transform) + (1.0 - gate) * layer_input.astype(F32)
        layer_input = mixed.astype(BF)
    part = tn(proj_weight, layer_input)
    encoded = (lax.psum_scatter(part.astype(BF), "enc", scatter_dimension=0, tiled=True)
               .astype(F32) + proj_bias[:, None]).astype(BF)
    outgoing = local(owner_pick, (owners * c, cap), [], asked, encoded)
    returned = lax.all_to_all(outgoing, "dp", split_axis=0, concat_axis=0, tiled=True)
    token_vectors = local(token_pick, (c, tokens), [], slot, returned).T

    def scatter_dp(x):
        n = lax.axis_size("dp")
        got = lax.all_to_all(x.astype(BF), "dp", split_axis=0, concat_axis=0, tiled=True)
        return jnp.sum(got.reshape((n, got.shape[0] // n) + got.shape[1:]).astype(F32), axis=0)

    d_projection = scatter_dp(nt(full_grads, layer_input)).T
    upstream = nn(proj_weight, full_grads)
    grads = [None] * layers
    for layer in reversed(range(layers)):
        layer_in, whole, transform, gate = saved[layer]
        rows = hw_weight[layer].reshape(total, 2 * filters)
        sigma = jax.nn.sigmoid(transform)
        slope = sigma * (1.0 + transform * (1.0 - sigma))
        d_transform = upstream * gate * slope
        d_gate = upstream * (transform * sigma - layer_in.astype(F32)) * gate * (1.0 - gate)
        pre_grads = jnp.concatenate([d_transform, d_gate], axis=0).astype(BF)
        back = nn(rows, pre_grads).astype(BF)
        grads[layer] = scatter_dp(nt(whole, pre_grads)).reshape(-1, 2, filters)
        upstream = upstream * (1.0 - gate) + lax.psum_scatter(
            back, "enc", scatter_dimension=0, tiled=True).astype(F32)
    return token_vectors, upstream.T.astype(BF), jnp.stack(grads), d_projection


def solution(mesh):
    return jax.shard_map(
        per_device,
        mesh=mesh,
        in_specs=(
            P("dp", None), P(), P(None, None, "enc"), P("enc"), P(None, None, None, "enc"),
            P(None, None, "enc"), P("enc", None), P("enc"), P("dp"), P("dp", None, None),
            P("dp"), P("dp", "enc"),
        ),
        out_specs=(P("dp", "enc"), P("dp", "enc"), P(None, "dp", None, "enc"), P("enc", "dp")),
        check_vma=False,
    )
```

```python
import functools
import jax
import jax.numpy as jnp
from jax import lax
from jax.experimental import pallas as pl
from jax.experimental.pallas import tpu as pltpu
from jax.sharding import PartitionSpec as P

BF = jnp.bfloat16
F32 = jnp.float32
VM = pl.BlockSpec(memory_space=pltpu.VMEM)
BASE = 128


def width_of(index, total):
    width = jnp.ones(index.shape, jnp.int32)
    for share in (1, 2, 4, 8, 16, 32):
        width = width + (index >= share * total // 64).astype(jnp.int32)
    return width


def one_hot(row, count):
    n = row.shape[1]
    return jnp.where(
        lax.broadcasted_iota(jnp.int32, (count, n), 0) == row, 1.0, 0.0
    ).astype(BF)


def nt(a, b):
    return lax.dot_general(a, b, (((1,), (1,)), ((), ())), preferred_element_type=F32)


def nn(a, b):
    return jnp.dot(a, b, preferred_element_type=F32)


def tn(a, b):
    return lax.dot_general(a, b, (((0,), (0,)), ((), ())), preferred_element_type=F32)


def column(row):
    return jnp.broadcast_to(row, (128, row.shape[1])).T[:, :1]


def encode_kernel(total, length, chars_ref, types_ref, table_ref, weight_ref, bias_ref,
                  out_ref, hot, lhs, acc, vec, band, best):
    step = pl.program_id(0)
    words = types_ref.shape[1]
    lanes = 256
    group = chars_ref.shape[1] // lanes
    rows = 64

    @pl.when(step == 0)
    def _():
        hot[...] = one_hot(types_ref[...] & (lanes - 1), lanes)
        acc[...] = jnp.zeros_like(acc)
        lhs[...] = jnp.zeros_like(lhs)

    high = types_ref[...] // lanes
    for part in range(group // 8):
        for j in range(8):
            block = chars_ref[:, (part * 8 + j) * lanes:(part * 8 + j + 1) * lanes]
            lhs[j * rows:j * rows + length, :] = (block - BASE).astype(F32).astype(BF)
        for half in range(words // 256):
            cols = slice(half * 256, half * 256 + 256)
            picked = nn(lhs[...], hot[:, cols])
            here = acc[:, cols]
            for j in range(8):
                here = jnp.where(high[:, cols] == step * group + part * 8 + j,
                                 picked[j * rows:(j + 1) * rows], here)
            acc[:, cols] = here

    @pl.when(step == pl.num_programs(0) - 1)
    def _():
        filters = weight_ref.shape[1]
        vec[length * 16:, :] = jnp.zeros((vec.shape[0] - length * 16, words), BF)

        def embed(p, carry):
            row = acc[pl.ds(p, 1), :].astype(jnp.int32) + BASE
            for b in range(words // 128):
                idx = jnp.broadcast_to(row[:, b * 128:(b + 1) * 128], (8, 128))
                low, seg = idx & 127, idx >> 7
                halves = []
                for h in range(2):
                    got = None
                    for s in range(3):
                        tab = table_ref[h * 8:(h + 1) * 8, s * 128:(s + 1) * 128]
                        val = jnp.take_along_axis(tab, low, axis=1)
                        got = val if got is None else jnp.where(seg == s, val, got)
                    halves.append(got)
                vec[pl.ds(pl.multiple_of(p * 16, 16), 16), b * 128:(b + 1) * 128] = (
                    jnp.concatenate(halves, axis=0).astype(BF))
            return carry

        lax.fori_loop(0, length, embed, 0)

        base = lax.axis_index("enc") * filters
        width_row = width_of(base + lax.broadcasted_iota(jnp.int32, (128, filters), 1), total)
        tap = lax.broadcasted_iota(jnp.int32, (128, filters), 0) // 16
        raw = jnp.concatenate(
            [weight_ref[...].astype(F32), jnp.zeros((128 - weight_ref.shape[0], filters), F32)],
            axis=0)
        kt = jnp.where(tap < width_row, raw, 0.0).T
        wide = jnp.concatenate([kt, jnp.zeros((filters, 128), F32)], axis=1)
        for q in range(8):
            moved = wide if q == 0 else pltpu.roll(wide, q * 16, 1)
            band[q * filters:(q + 1) * filters, :] = moved.astype(BF)
        best[...] = jnp.full(best.shape, -jnp.inf, F32)
        width_col = width_of(base + lax.broadcasted_iota(jnp.int32, (filters, 256), 0), total)
        groups = -(-length // 8)

        def conv(g, first, count, masked):
            for half in range(words // 256):
                cols = slice(half * 256, half * 256 + 256)
                win = vec[pl.ds(pl.multiple_of(g * 128, 128), 256), cols]
                out = nn(band[:count * filters, :], win)
                m = best[:, cols]
                for q in range(count):
                    val = out[q * filters:(q + 1) * filters]
                    if masked and first + q + 7 > length:
                        val = jnp.where(width_col <= length - first - q, val, -jnp.inf)
                    m = jnp.maximum(m, val)
                best[:, cols] = m

        def body(g, carry):
            conv(g, 0, 8, False)
            return carry

        lax.fori_loop(0, groups - 2, body, 0)
        for g in (groups - 2, groups - 1):
            conv(g, g * 8, min(8, length - g * 8), True)
        out_ref[...] = jnp.maximum(best[...] + column(bias_ref[...]), 0.0).astype(BF)


def encode(chars_t, types, table_t, weight, bias, total):
    length, count = chars_t.shape
    words = types.shape[1]
    filters = weight.shape[1]
    block = 4096
    return pl.pallas_call(
        functools.partial(encode_kernel, total, length),
        grid=(count // block,),
        in_specs=[pl.BlockSpec((length, block), lambda i: (0, i)), VM, VM, VM, VM],
        out_specs=VM,
        out_shape=jax.ShapeDtypeStruct((filters, words), BF),
        scratch_shapes=[
            pltpu.VMEM((256, words), BF),
            pltpu.VMEM((512, 256), BF),
            pltpu.VMEM((64, words), F32),
            pltpu.VMEM((1024, words), BF),
            pltpu.VMEM((8 * filters, 256), BF),
            pltpu.VMEM((filters, words), F32),
        ],
        compiler_params=pltpu.CompilerParams(vmem_limit_bytes=48 << 20),
    )(chars_t, types, table_t, weight, bias)


def slot_sums(slot_ref, d_ref, out_ref, acc, chunk=1024):
    c, tokens = d_ref.shape
    owners = out_ref.shape[0] // c
    acc[...] = jnp.zeros_like(acc)

    def body(i, carry):
        at = pl.ds(pl.multiple_of(i * chunk, chunk), chunk)
        slot = slot_ref[:, at]
        hot = one_hot(slot & 255, 256)
        high = slot >> 8
        d = d_ref[:, at]
        parts = [d * jnp.where(high == o, 1.0, 0.0).astype(BF) for o in range(owners)]
        acc[...] += nt(jnp.concatenate(parts, axis=0), hot)
        return carry

    lax.fori_loop(0, tokens // chunk, body, 0)
    out_ref[...] = acc[...].astype(BF)


def token_pick(slot_ref, ret_ref, out_ref, chunk=1024):
    c, tokens = out_ref.shape
    owners = ret_ref.shape[0] // c

    def body(i, carry):
        at = pl.ds(pl.multiple_of(i * chunk, chunk), chunk)
        slot = slot_ref[:, at]
        got = nn(ret_ref[...], one_hot(slot & 255, 256))
        high = slot >> 8
        out = jnp.zeros((c, chunk), F32)
        for o in range(owners):
            out = jnp.where(high == o, got[o * c:(o + 1) * c], out)
        out_ref[:, at] = out.astype(BF)
        return carry

    lax.fori_loop(0, tokens // chunk, body, 0)


def owner_sums(asked_ref, arr_ref, out_ref):
    c, unique = out_ref.shape
    reps, cap = asked_ref.shape
    acc = jnp.zeros((unique // 256 * c, 256), F32)
    for r in range(reps):
        asked = asked_ref[r:r + 1, :]
        hot = one_hot(asked & 255, 256)
        a = arr_ref[r * c:(r + 1) * c, :]
        parts = [a * jnp.where((asked >> 8) == h, 1.0, 0.0).astype(BF) for h in range(unique // 256)]
        acc += nt(jnp.concatenate(parts, axis=0), hot)
    for h in range(unique // 256):
        out_ref[:, h * 256:(h + 1) * 256] = acc[h * c:(h + 1) * c].astype(BF)


def owner_pick(asked_ref, enc_ref, out_ref):
    c, unique = enc_ref.shape
    reps, cap = asked_ref.shape
    enc = enc_ref[...]
    tall = jnp.concatenate([enc[:, h * 256:(h + 1) * 256] for h in range(unique // 256)], axis=0)
    for r in range(reps):
        asked = asked_ref[r:r + 1, :]
        got = nn(tall, one_hot(asked & 255, 256))
        out = jnp.zeros((c, cap), F32)
        for h in range(unique // 256):
            out = jnp.where((asked >> 8) == h, got[h * c:(h + 1) * c], out)
        out_ref[r * c:(r + 1) * c, :] = out.astype(BF)


def local(body, shape, scratch, *args):
    return pl.pallas_call(
        body, in_specs=[VM] * len(args), out_specs=VM,
        out_shape=jax.ShapeDtypeStruct(shape, BF), scratch_shapes=scratch,
        compiler_params=pltpu.CompilerParams(vmem_limit_bytes=48 << 20),
    )(*args)


MESH = pl.DeviceIdType.MESH


def send(src, dst, ssem, rsem, **to):
    return pltpu.make_async_remote_copy(
        src_ref=src, dst_ref=dst, send_sem=ssem, recv_sem=rsem, device_id=to, device_id_type=MESH)


def rows_at(ref, start, count):
    return ref.at[pl.ds(pl.multiple_of(start, count), count)]


class Place:
    def __init__(self):
        e = lax.axis_index("enc")
        self.chips = lax.axis_size("enc") // 2
        self.y, self.k = e // 2, lax.rem(e, 2)
        self.sib = self.y * 2 + 1 - self.k
        self.right = self.at(1)
        self.left = self.at(-1)

    def at(self, d, other=False):
        yy = lax.rem(self.y + d + self.chips, self.chips)
        return yy * 2 + (1 - self.k if other else self.k)


class Gather:
    def __init__(self, place, whole, rows, ssem, rsem, index):
        self.p, self.whole, self.rows = place, whole, rows
        self.s = lambda i: ssem.at[index, i]
        self.r = lambda i: rsem.at[index, i]

    def half(self, e, which):
        h = self.rows // 2
        return rows_at(self.whole, e * self.rows + which * h, h)

    def copy(self, i, ref, to):
        return send(ref, ref, self.s(i), self.r(i), enc=to)

    def start(self):
        p = self.p
        own = p.at(0)
        self.sends = [
            self.copy(0, self.half(own, 0), p.right),
            self.copy(1, self.half(own, 1), p.left),
            self.copy(2, self.half(own, 1), p.right),
            self.copy(3, self.half(own, 0), p.left),
            self.copy(4, rows_at(self.whole, own * self.rows, self.rows), p.sib),
        ]
        for c in self.sends:
            c.start()

    def more(self, i, ref, to):
        c = self.copy(i, ref, to)
        c.start()
        self.sends.append(c)

    def arrived(self, i, ref):
        self.copy(i, ref, self.p.sib).wait_recv()

    def forward1(self):
        p = self.p
        la, rb = self.half(p.at(-1), 0), self.half(p.at(1), 1)
        self.arrived(0, la)
        self.more(5, la, p.right)
        self.arrived(1, rb)
        self.more(6, rb, p.left)
        self.more(7, la, p.sib)
        self.more(8, rb, p.sib)

    def forward2(self):
        p = self.p
        lb, ra = self.half(p.at(-1), 1), self.half(p.at(1), 0)
        self.arrived(2, lb)
        self.more(9, lb, p.sib)
        self.arrived(3, ra)
        self.more(10, ra, p.sib)

    def wait_sib(self):
        self.arrived(4, rows_at(self.whole, self.p.sib * self.rows, self.rows))

    def forward3(self):
        p = self.p
        oa, ob = self.half(p.at(2), 0), self.half(p.at(2), 1)
        self.arrived(5, oa)
        self.more(11, oa, p.sib)
        self.arrived(6, ob)
        self.more(12, ob, p.sib)

    def finish_near(self):
        p = self.p
        for i, d, h in ((7, -1, 0), (8, 1, 1), (9, -1, 1), (10, 1, 0)):
            self.arrived(i, self.half(p.at(d, True), h))

    def finish_far(self):
        p = self.p
        for i, h in ((11, 0), (12, 1)):
            self.arrived(i, self.half(p.at(2, True), h))

    def drain(self):
        for c in self.sends:
            c.wait_send()


class Scatter:
    def __init__(self, place, rows, bufs, ssem, rsem, index):
        self.p, self.rows = place, rows
        self.sib_out, self.sib_in, self.ring, self.xin, self.lin, self.rin, self.own = bufs
        self.s = lambda i: ssem.at[index, i]
        self.r = lambda i: rsem.at[index, i]
        self.sends = []

    def go(self, i, src, dst, to):
        c = send(src, dst, self.s(i), self.r(i), enc=to)
        c.start()
        self.sends.append(c)

    def arrived(self, i, dst):
        send(dst, dst, self.s(i), self.r(i), enc=self.p.sib).wait_recv()

    def block(self, ref, d, which=None):
        if which is None:
            return ref.at[d * self.rows:(d + 1) * self.rows]
        h = self.rows // 2
        return ref.at[d * self.rows + which * h:d * self.rows + (which + 1) * h]

    def start(self, compute):
        p = self.p
        for d in (2, 1, 3, 0):
            self.block(self.sib_out, d)[...] = compute(p.at(d, True)).astype(BF)
            self.go(d, self.block(self.sib_out, d), self.block(self.sib_in, d), p.sib)
        for d in (2, 1, 3, 0):
            mine = compute(p.at(d))
            other = self.block(self.sib_in, d)
            self.arrived(d, other)
            mine = mine + other[...].astype(F32)
            if d == 0:
                self.own[...] = mine
                continue
            self.block(self.ring, d)[...] = mine.astype(BF)
            if d == 2:
                self.go(4, self.block(self.ring, 2, 0), self.block(self.xin, 0, 0), p.right)
                self.go(5, self.block(self.ring, 2, 1), self.block(self.xin, 0, 1), p.left)
            if d == 1:
                self.go(6, self.block(self.ring, 1, 1), self.block(self.lin, 0, 1), p.right)
            if d == 3:
                self.go(7, self.block(self.ring, 3, 0), self.block(self.rin, 0, 0), p.left)

    def mid(self):
        p = self.p
        for i, d, h, dst, to in ((4, 1, 0, self.lin, p.right), (5, 3, 1, self.rin, p.left)):
            came, mine = self.block(self.xin, 0, h), self.block(self.ring, d, h)
            self.arrived(i, came)
            mine[...] = (mine[...].astype(F32) + came[...].astype(F32)).astype(BF)
            self.go(i + 4, mine, self.block(dst, 0, h), to)

    def finish(self):
        self.arrived(6, self.block(self.lin, 0, 1))
        self.arrived(7, self.block(self.rin, 0, 0))
        self.arrived(8, self.block(self.lin, 0, 0))
        self.arrived(9, self.block(self.rin, 0, 1))

    def drain(self):
        for c in self.sends:
            c.wait_send()


def scatter_bufs(rows, n):
    return [((4 * rows, n), BF)] * 3 + [((rows, n), BF)] * 3 + [((rows, n), F32)]


class Exchange:
    def __init__(self, src, dst, rows, ssem, rsem, index):
        self.src, self.dst, self.rows = src, dst, rows
        self.n = lax.axis_size("dp")
        self.me = lax.axis_index("dp")
        self.ssem, self.rsem, self.index = ssem, rsem, index

    def at(self, ref, i):
        return ref.at[i] if self.rows is None else rows_at(ref, i * self.rows, self.rows)

    def copy(self, j):
        to = lax.rem(self.me + j, self.n)
        return send(self.at(self.src, to), self.at(self.dst, self.me),
                    self.ssem.at[self.index, j], self.rsem.at[self.index, j], dp=to)

    def start(self):
        def body(j, carry):
            self.copy(j).start()
            return carry
        lax.fori_loop(1, self.n, body, 0)
        self.at(self.dst, self.me)[...] = self.at(self.src, self.me)[...]

    def wait(self):
        def body(j, carry):
            came = self.at(self.dst, lax.rem(self.me - j + self.n, self.n))
            send(came, came, self.ssem.at[self.index, j], self.rsem.at[self.index, j],
                 dp=lax.rem(self.me + 1, self.n)).wait_recv()
            return carry
        lax.fori_loop(1, self.n, body, 0)

    def drain(self):
        def body(j, carry):
            self.copy(j).wait_send()
            return carry
        lax.fori_loop(1, self.n, body, 0)


def chunks(count, step, body):
    def run(i, carry):
        body(pl.ds(pl.multiple_of(i * step, step), step), i * step)
        return carry
    lax.fori_loop(0, count // step, run, 0)


INPUTS = ("features", "weight", "bias", "proj", "pbias", "slot", "d_tokens", "requests")
OUTPUTS = ("tokens", "d_features", "d_high", "d_proj")


def step_kernel(names, *refs):
    r = dict(zip(INPUTS + OUTPUTS + names, refs))
    place = Place()
    n_dp, me = lax.axis_size("dp"), lax.axis_index("dp")
    filters, words = r["features"].shape
    total = r["whole0"].shape[0]
    c, tokens = r["d_tokens"].shape
    cap = r["requests"].shape[2]
    e = place.at(0)

    barrier = pltpu.get_barrier_semaphore()
    for to in (place.left, place.right, place.sib):
        pl.semaphore_signal(barrier, inc=1, device_id={"enc": to}, device_id_type=MESH)

    def greet(j, carry):
        pl.semaphore_signal(barrier, inc=1, device_id={"dp": lax.rem(me + j, n_dp)},
                            device_id_type=MESH)
        return carry
    lax.fori_loop(1, n_dp, greet, 0)

    own_rows = pl.ds(pl.multiple_of(e * filters, filters), filters)
    r["whole0"][own_rows, :] = r["features"][...]
    pl.semaphore_wait(barrier, 3 + n_dp - 1)

    gather = [Gather(place, r["whole0"], filters, r["ag_s"], r["ag_r"], 0),
              Gather(place, r["whole1"], filters, r["ag_s"], r["ag_r"], 1),
              Gather(place, r["grads"], c, r["ag_s"], r["ag_r"], 2)]
    sums = [Scatter(place, filters, [r[f"rs{i}_{j}"] for j in range(7)], r["rs_s"], r["rs_r"], i)
            for i in range(2)]
    proj_sum = Scatter(place, c, [r[f"rs2_{j}"] for j in range(7)], r["rs_s"], r["rs_r"], 2)
    high_rows = total // n_dp
    proj_rows = r["proj"].shape[1] // n_dp

    def exchange(src, dst, rows, index):
        return Exchange(r[src], r[dst], rows, r["dp_s"], r["dp_r"], index)

    asked = exchange("requests", "asked", None, 0)
    slots = exchange("slot_out", "slot_in", c, 1)
    picked = exchange("pick_out", "pick_in", c, 2)
    d_proj = exchange("dp_out", "dp_in", proj_rows, 3)
    d_high = [exchange("dh0_out", "dh0_in", high_rows, 4), exchange("dh1_out", "dh1_in", high_rows, 5)]

    gather[0].start()
    asked.start()

    def layer(l, gat, whole, before, between, next_ref):
        acc, weight = r["acc"], r["weight"]

        def add(block, first=False):
            at = pl.ds(pl.multiple_of(block * filters, filters), filters)
            part = tn(weight[l, at, :], whole[at, :])
            acc[...] = part if first else acc[...] + part

        add(e, True)
        before()
        gat.forward1()
        between()
        gat.wait_sib()
        add(place.sib)
        gat.forward2()

        def near(i, carry):
            add(place.at(2 * i - 1))
            return carry
        lax.fori_loop(0, 2, near, 0)
        gat.forward3()
        add(place.at(2))
        gat.finish_near()

        def near_other(i, carry):
            add(place.at(2 * i - 1, True))
            return carry
        lax.fori_loop(0, 2, near_other, 0)
        gat.finish_far()
        add(place.at(2, True))
        bias = column(r["bias"][l:l + 1, :])
        r["bcol"][...] = jnp.broadcast_to(bias, (2 * filters, 128))

        def mix(at, start):
            low = pl.ds(pl.multiple_of(filters + start, 32), 32)
            t = acc[at, :] + jnp.tile(r["bcol"][at, :], (1, words // 128))
            g = jax.nn.sigmoid(acc[low, :] + jnp.tile(r["bcol"][low, :], (1, words // 128)))
            r["t"][l, at, :] = t
            r["g"][l, at, :] = g
            h = whole[pl.ds(pl.multiple_of(e * filters + start, 32), 32), :].astype(F32)
            out = (g * (t * jax.nn.sigmoid(t)) + (1.0 - g) * h).astype(BF)
            if next_ref is r["top"]:
                next_ref[at, :] = out
            else:
                next_ref[pl.ds(pl.multiple_of(e * filters + start, 32), 32), :] = out
        chunks(filters, 32, mix)
        gat.drain()

    n_chunks = tokens // 1024
    r["sacc"][...] = jnp.zeros_like(r["sacc"])

    def slot_part(first, last):
        def body(i, carry):
            at = pl.ds(pl.multiple_of(i * 1024, 1024), 1024)
            slot = r["slot"][:, at]
            hot = one_hot(slot & 255, 256)
            high = slot >> 8
            d = r["d_tokens"][:, at]
            parts = [d * jnp.where(high == o, 1.0, 0.0).astype(BF) for o in range(n_dp)]
            r["sacc"][...] += nt(jnp.concatenate(parts, axis=0), hot)
            return carry
        lax.fori_loop(first, last, body, 0)

    def slot_rest():
        slot_part(n_chunks // 2, n_chunks)
        r["slot_out"][...] = r["sacc"][...].astype(BF)
        slots.start()

    layer(0, gather[0], r["whole0"], lambda: slot_part(0, n_chunks // 2), slot_rest, r["whole1"])
    gather[1].start()
    asked.wait()
    for o in range(n_dp):
        r["asked2"][o:o + 1, :] = r["asked"][o]

    def owner_part():
        slots.wait()
        owner_sums(r["asked2"], r["slot_in"], r["row"])
        r["grads"][pl.ds(pl.multiple_of(e * c, c), c), :] = r["row"][...]
        gather[2].start()

    layer(1, gather[1], r["whole1"], lambda: None, owner_part, r["top"])

    top, proj = r["top"], r["proj"]
    width = r["proj"].shape[1]
    r["part"][...] = tn(proj[...], top[...])
    proj_sum.start(lambda dest: r["part"][pl.ds(pl.multiple_of(dest * c, c), c), :])
    gather[2].forward1()
    gather[2].forward2()
    gather[2].forward3()
    gather[2].wait_sib()
    gather[2].finish_near()
    gather[2].finish_far()
    up = r["up"]
    up[...] = nn(proj[...], r["grads"][...])
    proj_sum.mid()

    def cell(l):
        whole = r[f"whole{l}"]

        def body(at, start):
            t, g, u = r["t"][l, at, :], r["g"][l, at, :], up[at, :]
            h = whole[pl.ds(pl.multiple_of(e * filters + start, 32), 32), :].astype(F32)
            s = jax.nn.sigmoid(t)
            r["pre"][l, at, :] = (u * g * (s * (1.0 + t * (1.0 - s)))).astype(BF)
            low = pl.ds(pl.multiple_of(filters + start, 32), 32)
            r["pre"][l, low, :] = (u * (t * s - h) * g * (1.0 - g)).astype(BF)
            up[at, :] = u * (1.0 - g)
        chunks(filters, 32, body)

    def back(l):
        return lambda dest: nn(
            r["weight"][l, pl.ds(pl.multiple_of(dest * filters, filters), filters), :], r["pre"][l])

    def high_term(l):
        def body(at, start):
            r[f"dh{l}_out"][at, :] = nt(r[f"whole{l}"][at, :], r["pre"][l]).astype(BF)
        chunks(total, 256, body)
        d_high[l].start()

    def add_up(l, last):
        s = sums[l]

        def body(at, start):
            new = up[at, :] + (s.own[at, :] + s.lin[at, :].astype(F32) + s.rin[at, :].astype(F32))
            up[at, :] = new
        chunks(filters, 32, body)

    def high_sum(l):
        def body(at, start):
            got = jnp.zeros((32, 2 * filters), F32)
            for i in range(n_dp):
                got = got + r[f"dh{l}_in"][pl.ds(pl.multiple_of(i * high_rows + start, 32), 32), :].astype(F32)
            r["d_high"][l, at, :] = got
        d_high[l].wait()
        chunks(high_rows, 32, body)

    cell(1)
    sums[1].start(back(1))
    proj_sum.finish()
    r["encoded"][...] = (
        proj_sum.own[...] + proj_sum.lin[...].astype(F32) + proj_sum.rin[...].astype(F32)
        + column(r["pbias"][...])[:c]).astype(BF)
    owner_pick(r["asked2"], r["encoded"], r["pick_out"])
    picked.start()
    high_term(1)
    sums[1].mid()
    r["dp_out"][...] = nt(r["grads"][...], top[...]).astype(BF)
    d_proj.start()
    picked.wait()
    token_pick(r["slot"], r["pick_in"], r["tokens"])
    sums[1].finish()
    add_up(1, False)
    cell(0)
    high_term(0)
    sums[0].start(back(0))
    d_proj.wait()
    got = jnp.zeros((proj_rows, filters), F32)
    for i in range(n_dp):
        got = got + r["dp_in"][i * proj_rows:(i + 1) * proj_rows, :].astype(F32)
    r["d_proj"][...] = got
    high_sum(1)
    sums[0].mid()
    sums[0].finish()
    add_up(0, True)
    r["d_features"][...] = up[...].T.astype(BF)
    high_sum(0)
    for x in (asked, slots, picked, d_proj, d_high[0], d_high[1], gather[2], sums[0], sums[1], proj_sum):
        x.drain()


def step(features, weight, bias, proj, pbias, slot, d_tokens, requests, n_dp):
    filters, words = features.shape
    total = weight.shape[1]
    c, tokens = d_tokens.shape
    width = proj.shape[1]
    cap = requests.shape[2]
    bufs = {
        "whole0": ((total, words), BF), "whole1": ((total, words), BF), "grads": ((width, words), BF),
        "top": ((filters, words), BF), "acc": ((2 * filters, words), F32),
        "bcol": ((2 * filters, 128), F32),
        "t": ((2, filters, words), F32), "g": ((2, filters, words), F32),
        "pre": ((2, 2 * filters, words), BF), "up": ((filters, words), F32),
        "part": ((width, words), F32), "sacc": ((n_dp * c, cap), F32),
        "slot_out": ((n_dp * c, cap), BF), "slot_in": ((n_dp * c, cap), BF),
        "pick_out": ((n_dp * c, cap), BF), "pick_in": ((n_dp * c, cap), BF),
        "row": ((c, words), BF), "encoded": ((c, words), BF),
        "dp_out": ((width, filters), BF), "dp_in": ((width, filters), BF),
        "asked": ((n_dp, 1, cap), jnp.int32), "asked2": ((n_dp, cap), jnp.int32),
    }
    for l in range(2):
        for side in ("out", "in"):
            bufs[f"dh{l}_{side}"] = ((total, 2 * filters), BF)
    for i, rows in enumerate((filters, filters, c)):
        for j, spec in enumerate(scatter_bufs(rows, words)):
            bufs[f"rs{i}_{j}"] = spec
    scratch = [pltpu.VMEM(*spec) for spec in bufs.values()]
    sems = {"ag": (3, 13), "rs": (3, 10), "dp": (6, n_dp)}
    names = tuple(bufs)
    for name, dims in sems.items():
        names += (name + "_s", name + "_r")
        scratch += [pltpu.SemaphoreType.DMA(dims)] * 2
    return pl.pallas_call(
        functools.partial(step_kernel, names),
        in_specs=[VM] * len(INPUTS), out_specs=[VM] * len(OUTPUTS),
        out_shape=[
            jax.ShapeDtypeStruct((c, tokens), BF),
            jax.ShapeDtypeStruct((words, filters), BF),
            jax.ShapeDtypeStruct((2, total // n_dp, 2 * filters), F32),
            jax.ShapeDtypeStruct((width // n_dp, filters), F32),
        ],
        scratch_shapes=scratch,
        compiler_params=pltpu.CompilerParams(
            collective_id=0, has_side_effects=True, vmem_limit_bytes=62 << 20),
    )(features, weight, bias, proj, pbias, slot, d_tokens, requests)


def per_device(chars, char_table, conv_weight, conv_bias, hw_weight, hw_bias, proj_weight,
               proj_bias, owner_types, requests, tok_slot, d_tokens):
    taps, embed_width, filters = conv_weight.shape
    layers, total = hw_weight.shape[:2]
    unique = owner_types.shape[0]
    owners, cap = requests.shape[1:]
    tokens, c = d_tokens.shape
    table_t = jnp.pad(char_table.T.astype(F32), ((0, 0), (0, 384 - char_table.shape[0])))
    features = encode(chars.T, owner_types.reshape(1, unique), table_t,
                      conv_weight.reshape(taps * embed_width, filters),
                      conv_bias.reshape(1, filters), total)
    tok, d_feat, d_high, d_proj = step(
        features, hw_weight.reshape(layers, total, 2 * filters),
        hw_bias.reshape(layers, 2 * filters), proj_weight,
        jnp.pad(proj_bias.reshape(1, c), ((0, 0), (0, 128 - c))),
        tok_slot.reshape(1, tokens), d_tokens.T, requests.reshape(owners, 1, cap), owners)
    return tok.T, d_feat, d_high.reshape(layers, -1, 2, filters), d_proj.T


def solution(mesh):
    return jax.shard_map(
        per_device,
        mesh=mesh,
        in_specs=(
            P("dp", None), P(), P(None, None, "enc"), P("enc"), P(None, None, None, "enc"),
            P(None, None, "enc"), P("enc", None), P("enc"), P("dp"), P("dp", None, None),
            P("dp"), P("dp", "enc"),
        ),
        out_specs=(P("dp", "enc"), P("dp", "enc"), P(None, "dp", None, "enc"), P("enc", "dp")),
        check_vma=False,
    )
```

```python
import functools
import jax
import jax.numpy as jnp
from jax import lax
from jax.experimental import pallas as pl
from jax.experimental.pallas import tpu as pltpu
from jax.sharding import PartitionSpec as P

BF = jnp.bfloat16
F32 = jnp.float32
VM = pl.BlockSpec(memory_space=pltpu.VMEM)
BASE = 128


def width_of(index, total):
    width = jnp.ones(index.shape, jnp.int32)
    for share in (1, 2, 4, 8, 16, 32):
        width = width + (index >= share * total // 64).astype(jnp.int32)
    return width


def one_hot(row, count):
    n = row.shape[1]
    return jnp.where(
        lax.broadcasted_iota(jnp.int32, (count, n), 0) == row, 1.0, 0.0
    ).astype(BF)


def nt(a, b):
    return lax.dot_general(a, b, (((1,), (1,)), ((), ())), preferred_element_type=F32)


def nn(a, b):
    return jnp.dot(a, b, preferred_element_type=F32)


def tn(a, b):
    return lax.dot_general(a, b, (((0,), (0,)), ((), ())), preferred_element_type=F32)


def column(row):
    return jnp.broadcast_to(row, (128, row.shape[1])).T[:, :1]


def encode_kernel(total, length, chars_ref, types_ref, letters_ref, weight_ref, bias_ref,
                  out_ref, hot, lhs, acc, vec, band, best, table_ref):
    step = pl.program_id(0)
    words = types_ref.shape[1]
    lanes = 256
    group = chars_ref.shape[1] // lanes
    rows = 64

    @pl.when(step == 0)
    def _():
        hot[...] = one_hot(types_ref[...] & (lanes - 1), lanes)
        acc[...] = jnp.zeros_like(acc)
        lhs[...] = jnp.zeros_like(lhs)
        table_ref[...] = jnp.zeros_like(table_ref)
        table_ref[:, :letters_ref.shape[1]] = letters_ref[...].astype(F32)

    high = types_ref[...] // lanes
    for part in range(group // 8):
        for j in range(8):
            block = chars_ref[:, (part * 8 + j) * lanes:(part * 8 + j + 1) * lanes]
            lhs[j * rows:j * rows + length, :] = (block - BASE).astype(F32).astype(BF)
        for half in range(words // 256):
            cols = slice(half * 256, half * 256 + 256)
            picked = nn(lhs[...], hot[:, cols])
            here = acc[:, cols]
            for j in range(8):
                here = jnp.where(high[:, cols] == step * group + part * 8 + j,
                                 picked[j * rows:(j + 1) * rows], here)
            acc[:, cols] = here

    @pl.when(step == pl.num_programs(0) - 1)
    def _():
        filters = weight_ref.shape[1]
        vec[length * 16:, :] = jnp.zeros((vec.shape[0] - length * 16, words), BF)

        def embed(p, carry):
            row = acc[pl.ds(p, 1), :].astype(jnp.int32) + BASE
            for b in range(words // 128):
                idx = jnp.broadcast_to(row[:, b * 128:(b + 1) * 128], (8, 128))
                low, seg = idx & 127, idx >> 7
                halves = []
                for h in range(2):
                    got = None
                    for s in range(3):
                        tab = table_ref[h * 8:(h + 1) * 8, s * 128:(s + 1) * 128]
                        val = jnp.take_along_axis(tab, low, axis=1)
                        got = val if got is None else jnp.where(seg == s, val, got)
                    halves.append(got)
                vec[pl.ds(pl.multiple_of(p * 16, 16), 16), b * 128:(b + 1) * 128] = (
                    jnp.concatenate(halves, axis=0).astype(BF))
            return carry

        lax.fori_loop(0, length, embed, 0)

        base = lax.axis_index("enc") * filters
        width_row = width_of(base + lax.broadcasted_iota(jnp.int32, (128, filters), 1), total)
        tap = lax.broadcasted_iota(jnp.int32, (128, filters), 0) // 16
        raw = jnp.concatenate(
            [weight_ref[...].astype(F32), jnp.zeros((128 - weight_ref.shape[0], filters), F32)],
            axis=0)
        kt = jnp.where(tap < width_row, raw, 0.0).T
        wide = jnp.concatenate([kt, jnp.zeros((filters, 128), F32)], axis=1)
        for q in range(8):
            moved = wide if q == 0 else pltpu.roll(wide, q * 16, 1)
            band[q * filters:(q + 1) * filters, :] = moved.astype(BF)
        best[...] = jnp.full(best.shape, -jnp.inf, F32)
        width_col = width_of(base + lax.broadcasted_iota(jnp.int32, (filters, 256), 0), total)
        groups = -(-length // 8)

        def conv(g, first, count, masked):
            for half in range(words // 256):
                cols = slice(half * 256, half * 256 + 256)
                win = vec[pl.ds(pl.multiple_of(g * 128, 128), 256), cols]
                out = nn(band[:count * filters, :], win)
                m = best[:, cols]
                for q in range(count):
                    val = out[q * filters:(q + 1) * filters]
                    if masked and first + q + 7 > length:
                        val = jnp.where(width_col <= length - first - q, val, -jnp.inf)
                    m = jnp.maximum(m, val)
                best[:, cols] = m

        def body(g, carry):
            conv(g, 0, 8, False)
            return carry

        lax.fori_loop(0, groups - 2, body, 0)
        for g in (groups - 2, groups - 1):
            conv(g, g * 8, min(8, length - g * 8), True)
        out_ref[...] = jnp.maximum(best[...] + column(bias_ref[...]), 0.0).astype(BF)


def encode(chars_t, types, table_t, weight, bias, total):
    length, count = chars_t.shape
    words = types.shape[1]
    filters = weight.shape[1]
    block = 4096
    return pl.pallas_call(
        functools.partial(encode_kernel, total, length),
        grid=(count // block,),
        in_specs=[pl.BlockSpec((length, block), lambda i: (0, i)), VM, VM, VM, VM],
        out_specs=VM,
        out_shape=jax.ShapeDtypeStruct((filters, words), BF),
        scratch_shapes=[
            pltpu.VMEM((256, words), BF),
            pltpu.VMEM((512, 256), BF),
            pltpu.VMEM((64, words), F32),
            pltpu.VMEM((1024, words), BF),
            pltpu.VMEM((8 * filters, 256), BF),
            pltpu.VMEM((filters, words), F32),
            pltpu.VMEM((16, 384), F32),
        ],
        compiler_params=pltpu.CompilerParams(vmem_limit_bytes=48 << 20),
    )(chars_t, types, table_t, weight, bias)


def slot_sums(slot_ref, d_ref, out_ref, acc, chunk=1024):
    c, tokens = d_ref.shape
    owners = out_ref.shape[0] // c
    acc[...] = jnp.zeros_like(acc)

    def body(i, carry):
        at = pl.ds(pl.multiple_of(i * chunk, chunk), chunk)
        slot = slot_ref[:, at]
        hot = one_hot(slot & 255, 256)
        high = slot >> 8
        d = d_ref[:, at]
        parts = [d * jnp.where(high == o, 1.0, 0.0).astype(BF) for o in range(owners)]
        acc[...] += nt(jnp.concatenate(parts, axis=0), hot)
        return carry

    lax.fori_loop(0, tokens // chunk, body, 0)
    out_ref[...] = acc[...].astype(BF)


def token_pick(slot_ref, ret_ref, out_ref, chunk=1024):
    c, tokens = out_ref.shape
    owners = ret_ref.shape[0] // c

    def body(i, carry):
        at = pl.ds(pl.multiple_of(i * chunk, chunk), chunk)
        slot = slot_ref[:, at]
        got = nn(ret_ref[...], one_hot(slot & 255, 256))
        high = slot >> 8
        out = jnp.zeros((c, chunk), F32)
        for o in range(owners):
            out = jnp.where(high == o, got[o * c:(o + 1) * c], out)
        out_ref[:, at] = out.astype(BF)
        return carry

    lax.fori_loop(0, tokens // chunk, body, 0)


def owner_sums(asked_ref, arr_ref, out_ref):
    c, unique = out_ref.shape
    reps, cap = asked_ref.shape
    acc = jnp.zeros((unique // 256 * c, 256), F32)
    for r in range(reps):
        asked = asked_ref[r:r + 1, :]
        hot = one_hot(asked & 255, 256)
        a = arr_ref[r * c:(r + 1) * c, :]
        parts = [a * jnp.where((asked >> 8) == h, 1.0, 0.0).astype(BF) for h in range(unique // 256)]
        acc += nt(jnp.concatenate(parts, axis=0), hot)
    for h in range(unique // 256):
        out_ref[:, h * 256:(h + 1) * 256] = acc[h * c:(h + 1) * c].astype(BF)


def owner_pick(asked_ref, enc_ref, out_ref):
    c, unique = enc_ref.shape
    reps, cap = asked_ref.shape
    enc = enc_ref[...]
    tall = jnp.concatenate([enc[:, h * 256:(h + 1) * 256] for h in range(unique // 256)], axis=0)
    for r in range(reps):
        asked = asked_ref[r:r + 1, :]
        got = nn(tall, one_hot(asked & 255, 256))
        out = jnp.zeros((c, cap), F32)
        for h in range(unique // 256):
            out = jnp.where((asked >> 8) == h, got[h * c:(h + 1) * c], out)
        out_ref[r * c:(r + 1) * c, :] = out.astype(BF)


def local(body, shape, scratch, *args):
    return pl.pallas_call(
        body, in_specs=[VM] * len(args), out_specs=VM,
        out_shape=jax.ShapeDtypeStruct(shape, BF), scratch_shapes=scratch,
        compiler_params=pltpu.CompilerParams(vmem_limit_bytes=48 << 20),
    )(*args)


MESH = pl.DeviceIdType.MESH


def send(src, dst, ssem, rsem, **to):
    return pltpu.make_async_remote_copy(
        src_ref=src, dst_ref=dst, send_sem=ssem, recv_sem=rsem, device_id=to, device_id_type=MESH)


def rows_at(ref, start, count):
    return ref.at[pl.ds(pl.multiple_of(start, count), count)]


class Place:
    def __init__(self):
        e = lax.axis_index("enc")
        self.chips = lax.axis_size("enc") // 2
        self.y, self.k = e // 2, lax.rem(e, 2)
        self.sib = self.y * 2 + 1 - self.k
        self.right = self.at(1)
        self.left = self.at(-1)

    def at(self, d, other=False):
        yy = lax.rem(self.y + d + self.chips, self.chips)
        return yy * 2 + (1 - self.k if other else self.k)


class Gather:
    def __init__(self, place, whole, rows, ssem, rsem, index):
        self.p, self.whole, self.rows = place, whole, rows
        self.s = lambda i: ssem.at[index, i]
        self.r = lambda i: rsem.at[index, i]

    def half(self, e, which):
        h = self.rows // 2
        return rows_at(self.whole, e * self.rows + which * h, h)

    def copy(self, i, ref, to):
        return send(ref, ref, self.s(i), self.r(i), enc=to)

    def start(self):
        p = self.p
        own = p.at(0)
        self.sends = [
            self.copy(0, self.half(own, 0), p.right),
            self.copy(1, self.half(own, 1), p.left),
            self.copy(2, self.half(own, 1), p.right),
            self.copy(3, self.half(own, 0), p.left),
            self.copy(4, rows_at(self.whole, own * self.rows, self.rows), p.sib),
        ]
        for c in self.sends:
            c.start()

    def more(self, i, ref, to):
        c = self.copy(i, ref, to)
        c.start()
        self.sends.append(c)

    def arrived(self, i, ref):
        self.copy(i, ref, self.p.sib).wait_recv()

    def forward1(self):
        p = self.p
        la, rb = self.half(p.at(-1), 0), self.half(p.at(1), 1)
        self.arrived(0, la)
        self.more(5, la, p.right)
        self.arrived(1, rb)
        self.more(6, rb, p.left)
        self.more(7, la, p.sib)
        self.more(8, rb, p.sib)

    def forward2(self):
        p = self.p
        lb, ra = self.half(p.at(-1), 1), self.half(p.at(1), 0)
        self.arrived(2, lb)
        self.more(9, lb, p.sib)
        self.arrived(3, ra)
        self.more(10, ra, p.sib)

    def wait_sib(self):
        self.arrived(4, rows_at(self.whole, self.p.sib * self.rows, self.rows))

    def forward3(self):
        p = self.p
        oa, ob = self.half(p.at(2), 0), self.half(p.at(2), 1)
        self.arrived(5, oa)
        self.more(11, oa, p.sib)
        self.arrived(6, ob)
        self.more(12, ob, p.sib)

    def finish_near(self):
        p = self.p
        for i, d, h in ((7, -1, 0), (8, 1, 1), (9, -1, 1), (10, 1, 0)):
            self.arrived(i, self.half(p.at(d, True), h))

    def finish_far(self):
        p = self.p
        for i, h in ((11, 0), (12, 1)):
            self.arrived(i, self.half(p.at(2, True), h))

    def drain(self):
        for c in self.sends:
            c.wait_send()


class Scatter:
    def __init__(self, place, rows, bufs, ssem, rsem, index):
        self.p, self.rows = place, rows
        self.sib_out, self.sib_in, self.ring, self.xin, self.lin, self.rin, self.own = bufs
        self.s = lambda i: ssem.at[index, i]
        self.r = lambda i: rsem.at[index, i]
        self.sends = []

    def go(self, i, src, dst, to):
        c = send(src, dst, self.s(i), self.r(i), enc=to)
        c.start()
        self.sends.append(c)

    def arrived(self, i, dst):
        send(dst, dst, self.s(i), self.r(i), enc=self.p.sib).wait_recv()

    def block(self, ref, d, which=None):
        if which is None:
            return ref.at[d * self.rows:(d + 1) * self.rows]
        h = self.rows // 2
        return ref.at[d * self.rows + which * h:d * self.rows + (which + 1) * h]

    def start(self, compute):
        p = self.p
        for d in (2, 1, 3, 0):
            self.block(self.sib_out, d)[...] = compute(p.at(d, True)).astype(BF)
            self.go(d, self.block(self.sib_out, d), self.block(self.sib_in, d), p.sib)
        for d in (2, 1, 3, 0):
            mine = compute(p.at(d))
            other = self.block(self.sib_in, d)
            self.arrived(d, other)
            mine = mine + other[...].astype(F32)
            if d == 0:
                self.own[...] = mine
                continue
            self.block(self.ring, d)[...] = mine.astype(BF)
            if d == 2:
                self.go(4, self.block(self.ring, 2, 0), self.block(self.xin, 0, 0), p.right)
                self.go(5, self.block(self.ring, 2, 1), self.block(self.xin, 0, 1), p.left)
            if d == 1:
                self.go(6, self.block(self.ring, 1, 1), self.block(self.lin, 0, 1), p.right)
            if d == 3:
                self.go(7, self.block(self.ring, 3, 0), self.block(self.rin, 0, 0), p.left)

    def mid(self):
        p = self.p
        for i, d, h, dst, to in ((4, 1, 0, self.lin, p.right), (5, 3, 1, self.rin, p.left)):
            came, mine = self.block(self.xin, 0, h), self.block(self.ring, d, h)
            self.arrived(i, came)
            mine[...] = (mine[...].astype(F32) + came[...].astype(F32)).astype(BF)
            self.go(i + 4, mine, self.block(dst, 0, h), to)

    def finish(self):
        self.arrived(6, self.block(self.lin, 0, 1))
        self.arrived(7, self.block(self.rin, 0, 0))
        self.arrived(8, self.block(self.lin, 0, 0))
        self.arrived(9, self.block(self.rin, 0, 1))

    def drain(self):
        for c in self.sends:
            c.wait_send()


def scatter_bufs(rows, n):
    return [((4 * rows, n), BF)] * 3 + [((rows, n), BF)] * 3 + [((rows, n), F32)]


class Exchange:
    def __init__(self, src, dst, rows, ssem, rsem, index):
        self.src, self.dst, self.rows = src, dst, rows
        self.n = lax.axis_size("dp")
        self.me = lax.axis_index("dp")
        self.ssem, self.rsem, self.index = ssem, rsem, index

    def at(self, ref, i):
        return ref.at[i] if self.rows is None else rows_at(ref, i * self.rows, self.rows)

    def copy(self, j):
        to = lax.rem(self.me + j, self.n)
        return send(self.at(self.src, to), self.at(self.dst, self.me),
                    self.ssem.at[self.index, j], self.rsem.at[self.index, j], dp=to)

    def start(self):
        def body(j, carry):
            self.copy(j).start()
            return carry
        lax.fori_loop(1, self.n, body, 0)
        self.at(self.dst, self.me)[...] = self.at(self.src, self.me)[...]

    def wait(self):
        def body(j, carry):
            came = self.at(self.dst, lax.rem(self.me - j + self.n, self.n))
            send(came, came, self.ssem.at[self.index, j], self.rsem.at[self.index, j],
                 dp=lax.rem(self.me + 1, self.n)).wait_recv()
            return carry
        lax.fori_loop(1, self.n, body, 0)

    def drain(self):
        def body(j, carry):
            self.copy(j).wait_send()
            return carry
        lax.fori_loop(1, self.n, body, 0)


def chunks(count, step, body):
    def run(i, carry):
        body(pl.ds(pl.multiple_of(i * step, step), step), i * step)
        return carry
    lax.fori_loop(0, count // step, run, 0)


INPUTS = ("features", "weight_in", "bias", "proj", "pbias", "slot", "d_tokens", "requests")
OUTPUTS = ("tokens", "d_features", "d_high", "d_proj")


def step_kernel(names, *refs):
    r = dict(zip(INPUTS + OUTPUTS + names, refs))
    place = Place()
    n_dp, me = lax.axis_size("dp"), lax.axis_index("dp")
    filters, words = r["features"].shape
    total = r["whole0"].shape[0]
    c, tokens = r["d_tokens"].shape
    cap = r["requests"].shape[1]
    e = place.at(0)
    raw = pltpu.make_async_copy(r["weight_in"].at[0], r["raw"], r["raw_s"].at[0])
    raw.start()
    for o in range(n_dp):
        r["wanted"][o] = r["requests"][o:o + 1, :]

    barrier = pltpu.get_barrier_semaphore()
    for to in (place.left, place.right, place.sib):
        pl.semaphore_signal(barrier, inc=1, device_id={"enc": to}, device_id_type=MESH)

    def greet(j, carry):
        pl.semaphore_signal(barrier, inc=1, device_id={"dp": lax.rem(me + j, n_dp)},
                            device_id_type=MESH)
        return carry
    lax.fori_loop(1, n_dp, greet, 0)

    own_rows = pl.ds(pl.multiple_of(e * filters, filters), filters)
    r["whole0"][own_rows, :] = r["features"][...]
    pl.semaphore_wait(barrier, 3 + n_dp - 1)

    gather = [Gather(place, r["whole0"], filters, r["ag_s"], r["ag_r"], 0),
              Gather(place, r["whole1"], filters, r["ag_s"], r["ag_r"], 1),
              Gather(place, r["grads"], c, r["ag_s"], r["ag_r"], 2)]
    sums = [Scatter(place, filters, [r[f"rs{0 if j in (0, 2) else i}_{j}"] for j in range(7)], r["rs_s"], r["rs_r"], i)
            for i in range(2)]
    proj_sum = Scatter(place, c, [r[f"rs2_{j}"] for j in range(7)], r["rs_s"], r["rs_r"], 2)
    high_rows = total // n_dp
    proj_rows = r["proj"].shape[1] // n_dp

    def exchange(src, dst, rows, index):
        return Exchange(r[src], r[dst], rows, r["dp_s"], r["dp_r"], index)

    asked = exchange("wanted", "asked", None, 0)
    slots = exchange("slot_out", "slot_in", c, 1)
    picked = exchange("pick_out", "pick_in", c, 2)
    d_proj = exchange("dp_out", "dp_in", proj_rows, 3)
    d_high = [exchange("dh0_out", "dh0_in", high_rows, 4), exchange("dh1_out", "dh1_in", high_rows, 5)]

    gather[0].start()
    asked.start()

    def unpack(l):
        raw.wait()

        def body(at, start):
            r["weight"][l, at, :] = r["raw"][at].reshape(64, 2 * filters)
        chunks(total, 64, body)

    unpack(0)
    raw = pltpu.make_async_copy(r["weight_in"].at[1], r["raw"], r["raw_s"].at[1])
    raw.start()

    def layer(l, gat, whole, before, between, next_ref):
        acc, weight = r["acc"], r["weight"]

        def add(block, first=False):
            at = pl.ds(pl.multiple_of(block * filters, filters), filters)
            part = tn(weight[l, at, :], whole[at, :])
            acc[...] = part if first else acc[...] + part

        if l == 1:
            unpack(1)
        add(e, True)
        if before is not None:
            before()
        gat.forward1()
        between()
        gat.wait_sib()
        add(place.sib)
        gat.forward2()

        def near(i, carry):
            add(place.at(2 * i - 1))
            return carry
        lax.fori_loop(0, 2, near, 0)
        gat.forward3()
        add(place.at(2))
        gat.finish_near()

        def near_other(i, carry):
            add(place.at(2 * i - 1, True))
            return carry
        lax.fori_loop(0, 2, near_other, 0)
        gat.finish_far()
        add(place.at(2, True))
        for i in range(2):
            r["bcol"][i * filters:(i + 1) * filters, :] = jnp.broadcast_to(
                r["bias"][l, i:i + 1, :], (128, filters)).T

        def mix(at, start):
            low = pl.ds(pl.multiple_of(filters + start, 32), 32)
            t = acc[at, :] + jnp.tile(r["bcol"][at, :], (1, words // 128))
            g = jax.nn.sigmoid(acc[low, :] + jnp.tile(r["bcol"][low, :], (1, words // 128)))
            r["t"][l, at, :] = t
            r["g"][l, at, :] = g
            h = whole[pl.ds(pl.multiple_of(e * filters + start, 32), 32), :].astype(F32)
            out = (g * (t * jax.nn.sigmoid(t)) + (1.0 - g) * h).astype(BF)
            if next_ref is r["top"]:
                next_ref[at, :] = out
            else:
                next_ref[pl.ds(pl.multiple_of(e * filters + start, 32), 32), :] = out
        chunks(filters, 32, mix)
        gat.drain()

    n_chunks = tokens // 1024
    r["sacc"][...] = jnp.zeros_like(r["sacc"])

    def slot_part(first, last):
        def body(i, carry):
            at = pl.ds(pl.multiple_of(i * 1024, 1024), 1024)
            slot = r["slot"][:, at]
            hot = one_hot(slot & 255, 256)
            high = slot >> 8
            d = r["d_tokens"][:, at]
            parts = [d * jnp.where(high == o, 1.0, 0.0).astype(BF) for o in range(n_dp)]
            r["sacc"][...] += nt(jnp.concatenate(parts, axis=0), hot)
            return carry
        lax.fori_loop(first, last, body, 0)

    def slot_rest():
        slot_part(n_chunks // 2, n_chunks)
        r["slot_out"][...] = r["sacc"][...].astype(BF)
        slots.start()

    layer(0, gather[0], r["whole0"], lambda: slot_part(0, n_chunks // 2), slot_rest, r["whole1"])
    gather[1].start()
    asked.wait()
    for o in range(n_dp):
        r["asked2"][o:o + 1, :] = r["asked"][o]

    def owner_part():
        slots.wait()
        owner_sums(r["asked2"], r["slot_in"], r["row"])
        r["grads"][pl.ds(pl.multiple_of(e * c, c), c), :] = r["row"][...]
        gather[2].start()

    layer(1, gather[1], r["whole1"], None, owner_part, r["top"])

    top, proj = r["top"], r["proj"]
    width = r["proj"].shape[1]
    r["acc"][...] = tn(proj[...], top[...])
    proj_sum.start(lambda dest: r["acc"][pl.ds(pl.multiple_of(dest * c, c), c), :])
    gather[2].forward1()
    gather[2].forward2()
    gather[2].forward3()
    gather[2].wait_sib()
    gather[2].finish_near()
    gather[2].finish_far()
    up = r["up"]
    up[...] = nn(proj[...], r["grads"][...])
    proj_sum.mid()

    def cell(l):
        whole = r[f"whole{l}"]

        def body(at, start):
            t, g, u = r["t"][l, at, :], r["g"][l, at, :], up[at, :]
            h = whole[pl.ds(pl.multiple_of(e * filters + start, 32), 32), :].astype(F32)
            s = jax.nn.sigmoid(t)
            r["pre"][l, at, :] = (u * g * (s * (1.0 + t * (1.0 - s)))).astype(BF)
            low = pl.ds(pl.multiple_of(filters + start, 32), 32)
            r["pre"][l, low, :] = (u * (t * s - h) * g * (1.0 - g)).astype(BF)
            up[at, :] = u * (1.0 - g)
        chunks(filters, 32, body)

    def back(l):
        return lambda dest: nn(
            r["weight"][l, pl.ds(pl.multiple_of(dest * filters, filters), filters), :], r["pre"][l])

    def high_term(l):
        def body(at, start):
            r[f"dh{l}_out"][at, :] = nt(r[f"whole{l}"][at, :], r["pre"][l]).astype(BF)
        chunks(total, 256, body)
        d_high[l].start()

    def add_up(l, last):
        s = sums[l]

        def body(at, start):
            new = up[at, :] + (s.own[at, :] + s.lin[at, :].astype(F32) + s.rin[at, :].astype(F32))
            up[at, :] = new
        chunks(filters, 32, body)

    def high_sum(l):
        def body(at, start):
            got = jnp.zeros((32, 2 * filters), F32)
            for i in range(n_dp):
                got = got + r[f"dh{l}_in"][pl.ds(pl.multiple_of(i * high_rows + start, 32), 32), :].astype(F32)
            r["d_high"][l, at, 0, :] = got[:, :filters]
            r["d_high"][l, at, 1, :] = got[:, filters:]
        d_high[l].wait()
        chunks(high_rows, 32, body)

    cell(1)
    sums[1].start(back(1))
    proj_sum.finish()
    r["encoded"][...] = (
        proj_sum.own[...] + proj_sum.lin[...].astype(F32) + proj_sum.rin[...].astype(F32)
        + column(jnp.concatenate([r["pbias"][...], jnp.zeros((1, 128 - c), F32)], axis=1))[:c]).astype(BF)
    owner_pick(r["asked2"], r["encoded"], r["pick_out"])
    picked.start()
    high_term(1)
    sums[1].mid()
    r["dp_out"][...] = nt(r["grads"][...], top[...]).astype(BF)
    d_proj.start()
    picked.wait()
    token_pick(r["slot"], r["pick_in"], r["tokens"])
    sums[1].finish()
    add_up(1, False)
    cell(0)
    high_term(0)
    sums[1].drain()
    sums[0].start(back(0))
    d_proj.wait()
    got = jnp.zeros((proj_rows, filters), F32)
    for i in range(n_dp):
        got = got + r["dp_in"][i * proj_rows:(i + 1) * proj_rows, :].astype(F32)
    r["d_proj"][...] = got
    high_sum(1)
    sums[0].mid()
    sums[0].finish()
    add_up(0, True)
    r["d_features"][...] = up[...].T.astype(BF)
    high_sum(0)
    for x in (asked, slots, picked, d_proj, d_high[0], d_high[1], gather[2], sums[0], proj_sum):
        x.drain()


def step(features, weight, bias, proj, pbias, slot, d_tokens, requests, n_dp):
    filters, words = features.shape
    total = weight.shape[1]
    c, tokens = d_tokens.shape
    width = proj.shape[1]
    cap = requests.shape[1]
    bufs = {
        "whole0": ((total, words), BF), "whole1": ((total, words), BF), "grads": ((width, words), BF),
        "top": ((filters, words), BF), "acc": ((2 * filters, words), F32),
        "bcol": ((2 * filters, 128), F32),
        "t": ((2, filters, words), F32), "g": ((2, filters, words), F32),
        "pre": ((2, 2 * filters, words), BF), "up": ((filters, words), F32),
        "sacc": ((n_dp * c, cap), F32),
        "slot_out": ((n_dp * c, cap), BF), "slot_in": ((n_dp * c, cap), BF),
        "pick_out": ((n_dp * c, cap), BF), "pick_in": ((n_dp * c, cap), BF),
        "row": ((c, words), BF), "encoded": ((c, words), BF),
        "dp_out": ((width, filters), BF), "dp_in": ((width, filters), BF),
        "weight": ((2, total, 2 * filters), BF), "raw": ((total, 2, filters), BF),
        "wanted": ((n_dp, 1, cap), jnp.int32), "asked": ((n_dp, 1, cap), jnp.int32), "asked2": ((n_dp, cap), jnp.int32),
    }
    for l in range(2):
        for side in ("out", "in"):
            bufs[f"dh{l}_{side}"] = ((total, 2 * filters), BF)
    for i, rows in enumerate((filters, filters, c)):
        for j, spec in enumerate(scatter_bufs(rows, words)):
            if i != 1 or j not in (0, 2):
                bufs[f"rs{i}_{j}"] = spec
    scratch = [pltpu.VMEM(*spec) for spec in bufs.values()]
    sems = {"ag": (3, 13), "rs": (3, 10), "dp": (6, n_dp), "raw": (2,)}
    names = tuple(bufs)
    for name, dims in sems.items():
        names += (name + "_s", name + "_r")
        scratch += [pltpu.SemaphoreType.DMA(dims)] * 2
    return pl.pallas_call(
        functools.partial(step_kernel, names),
        in_specs=[pl.BlockSpec(memory_space=pl.ANY) if x == "weight_in" else VM for x in INPUTS], out_specs=[VM] * len(OUTPUTS),
        out_shape=[
            jax.ShapeDtypeStruct((c, tokens), BF),
            jax.ShapeDtypeStruct((words, filters), BF),
            jax.ShapeDtypeStruct((2, total // n_dp, 2, filters), F32),
            jax.ShapeDtypeStruct((width // n_dp, filters), F32),
        ],
        scratch_shapes=scratch,
        compiler_params=pltpu.CompilerParams(
            collective_id=0, has_side_effects=True, vmem_limit_bytes=62 << 20),
    )(features, weight, bias, proj, pbias, slot, d_tokens, requests)


def hand_on(*arrays):
    n = len(arrays)

    def kernel(*refs):
        for i in range(n):
            refs[n + i][...] = refs[i][...]

    return pl.pallas_call(
        kernel, in_specs=[VM] * n, out_specs=[VM] * n,
        out_shape=[jax.ShapeDtypeStruct(a.shape, a.dtype) for a in arrays],
        compiler_params=pltpu.CompilerParams(vmem_limit_bytes=32 << 20),
    )(*arrays)


def per_device(chars, char_table, conv_weight, conv_bias, hw_weight, hw_bias, proj_weight,
               proj_bias, owner_types, requests, tok_slot, d_tokens):
    taps, embed_width, filters = conv_weight.shape
    layers, total = hw_weight.shape[:2]
    unique = owner_types.shape[0]
    owners, cap = requests.shape[1:]
    tokens, c = d_tokens.shape
    features = encode(chars.T, owner_types.reshape(1, unique), char_table.T,
                      conv_weight.reshape(taps * embed_width, filters),
                      conv_bias.reshape(1, filters), total)
    outs = step(
        features, hw_weight, hw_bias, proj_weight, proj_bias.reshape(1, c),
        tok_slot.reshape(1, tokens), d_tokens.T, requests.reshape(owners, cap), owners)
    tok, d_feat, d_high, d_proj = hand_on(*outs)
    return tok.T, d_feat, d_high, d_proj.T


def solution(mesh):
    return jax.shard_map(
        per_device,
        mesh=mesh,
        in_specs=(
            P("dp", None), P(), P(None, None, "enc"), P("enc"), P(None, None, None, "enc"),
            P(None, None, "enc"), P("enc", None), P("enc"), P("dp"), P("dp", None, None),
            P("dp"), P("dp", "enc"),
        ),
        out_specs=(P("dp", "enc"), P("dp", "enc"), P(None, "dp", None, "enc"), P("enc", "dp")),
        check_vma=False,
    )
```

```python
import math
import functools
import jax
import jax.numpy as jnp
from jax import lax
from jax.experimental import pallas as pl
from jax.experimental.pallas import tpu as pltpu
from jax.sharding import PartitionSpec as P

BF = jnp.bfloat16
F32 = jnp.float32
VM = pl.BlockSpec(memory_space=pltpu.VMEM)
BASE = 128


def width_of(index, total):
    width = jnp.ones(index.shape, jnp.int32)
    for share in (1, 2, 4, 8, 16, 32):
        width = width + (index >= share * total // 64).astype(jnp.int32)
    return width


def one_hot(row, count):
    n = row.shape[1]
    return jnp.where(
        lax.broadcasted_iota(jnp.int32, (count, n), 0) == row, 1.0, 0.0
    ).astype(BF)


def nt(a, b):
    return lax.dot_general(a, b, (((1,), (1,)), ((), ())), preferred_element_type=F32)


def nn(a, b):
    return jnp.dot(a, b, preferred_element_type=F32)


def tn(a, b):
    return lax.dot_general(a, b, (((0,), (0,)), ((), ())), preferred_element_type=F32)


def column(row):
    return jnp.broadcast_to(row, (128, row.shape[1])).T[:, :1]


def encode_kernel(total, length, chars_ref, types_ref, letters_ref, weight_ref, bias_ref,
                  out_ref, hot, lhs, acc, vec, band, best, table_ref):
    step = pl.program_id(0)
    words = types_ref.shape[1]
    lanes = 256
    group = chars_ref.shape[1] // lanes
    rows = 64

    @pl.when(step == 0)
    def _():
        hot[...] = one_hot(types_ref[...] & (lanes - 1), lanes)
        acc[...] = jnp.zeros_like(acc)
        lhs[...] = jnp.zeros_like(lhs)
        table_ref[...] = jnp.zeros_like(table_ref)
        table_ref[:, :letters_ref.shape[1]] = letters_ref[...].astype(F32)

    high = types_ref[...] // lanes
    for part in range(group // 8):
        for j in range(8):
            block = chars_ref[:, (part * 8 + j) * lanes:(part * 8 + j + 1) * lanes]
            lhs[j * rows:j * rows + length, :] = (block - BASE).astype(F32).astype(BF)
        for half in range(words // 256):
            cols = slice(half * 256, half * 256 + 256)
            picked = nn(lhs[...], hot[:, cols])
            here = acc[:, cols]
            for j in range(8):
                here = jnp.where(high[:, cols] == step * group + part * 8 + j,
                                 picked[j * rows:(j + 1) * rows], here)
            acc[:, cols] = here

    @pl.when(step == pl.num_programs(0) - 1)
    def _():
        filters = weight_ref.shape[1]
        vec[length * 16:, :] = jnp.zeros((vec.shape[0] - length * 16, words), BF)

        def embed(p, carry):
            row = acc[pl.ds(p, 1), :].astype(jnp.int32) + BASE
            for b in range(words // 128):
                idx = jnp.broadcast_to(row[:, b * 128:(b + 1) * 128], (8, 128))
                low, seg = idx & 127, idx >> 7
                halves = []
                for h in range(2):
                    got = None
                    for s in range(3):
                        tab = table_ref[h * 8:(h + 1) * 8, s * 128:(s + 1) * 128]
                        val = jnp.take_along_axis(tab, low, axis=1)
                        got = val if got is None else jnp.where(seg == s, val, got)
                    halves.append(got)
                vec[pl.ds(pl.multiple_of(p * 16, 16), 16), b * 128:(b + 1) * 128] = (
                    jnp.concatenate(halves, axis=0).astype(BF))
            return carry

        lax.fori_loop(0, length, embed, 0)

        base = lax.axis_index("enc") * filters
        width_row = width_of(base + lax.broadcasted_iota(jnp.int32, (128, filters), 1), total)
        tap = lax.broadcasted_iota(jnp.int32, (128, filters), 0) // 16
        raw = jnp.concatenate(
            [weight_ref[...].astype(F32), jnp.zeros((128 - weight_ref.shape[0], filters), F32)],
            axis=0)
        kt = jnp.where(tap < width_row, raw, 0.0).T
        wide = jnp.concatenate([kt, jnp.zeros((filters, 128), F32)], axis=1)
        for q in range(8):
            moved = wide if q == 0 else pltpu.roll(wide, q * 16, 1)
            band[q * filters:(q + 1) * filters, :] = moved.astype(BF)
        best[...] = jnp.full(best.shape, -jnp.inf, F32)
        width_col = width_of(base + lax.broadcasted_iota(jnp.int32, (filters, 256), 0), total)
        groups = -(-length // 8)

        def conv(g, first, count, masked):
            for half in range(words // 256):
                cols = slice(half * 256, half * 256 + 256)
                win = vec[pl.ds(pl.multiple_of(g * 128, 128), 256), cols]
                out = nn(band[:count * filters, :], win)
                m = best[:, cols]
                for q in range(count):
                    val = out[q * filters:(q + 1) * filters]
                    if masked and first + q + 7 > length:
                        val = jnp.where(width_col <= length - first - q, val, -jnp.inf)
                    m = jnp.maximum(m, val)
                best[:, cols] = m

        def body(g, carry):
            conv(g, 0, 8, False)
            return carry

        lax.fori_loop(0, groups - 2, body, 0)
        for g in (groups - 2, groups - 1):
            conv(g, g * 8, min(8, length - g * 8), True)
        out_ref[...] = jnp.maximum(best[...] + column(bias_ref[...]), 0.0).astype(BF)


def encode(chars_t, types, table_t, weight, bias, total):
    length, count = chars_t.shape
    words = types.shape[1]
    filters = weight.shape[1]
    block = 4096
    return pl.pallas_call(
        functools.partial(encode_kernel, total, length),
        grid=(count // block,),
        in_specs=[pl.BlockSpec((length, block), lambda i: (0, i)), VM, VM, VM, VM],
        out_specs=VM,
        out_shape=jax.ShapeDtypeStruct((filters, words), BF),
        scratch_shapes=[
            pltpu.VMEM((256, words), BF),
            pltpu.VMEM((512, 256), BF),
            pltpu.VMEM((64, words), F32),
            pltpu.VMEM((1024, words), BF),
            pltpu.VMEM((8 * filters, 256), BF),
            pltpu.VMEM((filters, words), F32),
            pltpu.VMEM((16, 384), F32),
        ],
        compiler_params=pltpu.CompilerParams(vmem_limit_bytes=63 << 20),
    )(chars_t, types, table_t, weight, bias)


def slot_sums(slot_ref, d_ref, out_ref, acc, chunk=1024):
    c, tokens = d_ref.shape
    owners = out_ref.shape[0] // c
    acc[...] = jnp.zeros_like(acc)

    def body(i, carry):
        at = pl.ds(pl.multiple_of(i * chunk, chunk), chunk)
        slot = slot_ref[:, at]
        hot = one_hot(slot & 255, 256)
        high = slot >> 8
        d = d_ref[:, at]
        parts = [d * jnp.where(high == o, 1.0, 0.0).astype(BF) for o in range(owners)]
        acc[...] += nt(jnp.concatenate(parts, axis=0), hot)
        return carry

    lax.fori_loop(0, tokens // chunk, body, 0)
    out_ref[...] = acc[...].astype(BF)


def token_pick(slot_ref, ret_ref, out_ref, chunk=1024):
    c, tokens = out_ref.shape
    owners = ret_ref.shape[0] // c

    def body(i, carry):
        at = pl.ds(pl.multiple_of(i * chunk, chunk), chunk)
        slot = slot_ref[:, at]
        got = nn(ret_ref[...], one_hot(slot & 255, 256))
        high = slot >> 8
        out = jnp.zeros((c, chunk), F32)
        for o in range(owners):
            out = jnp.where(high == o, got[o * c:(o + 1) * c], out)
        out_ref[:, at] = out.astype(BF)
        return carry

    lax.fori_loop(0, tokens // chunk, body, 0)


def owner_sums(asked_ref, arr_ref, out_ref):
    c, unique = out_ref.shape
    reps, cap = asked_ref.shape
    acc = jnp.zeros((unique // 256 * c, 256), F32)
    for r in range(reps):
        asked = asked_ref[r:r + 1, :]
        hot = one_hot(asked & 255, 256)
        a = arr_ref[r * c:(r + 1) * c, :]
        parts = [a * jnp.where((asked >> 8) == h, 1.0, 0.0).astype(BF) for h in range(unique // 256)]
        acc += nt(jnp.concatenate(parts, axis=0), hot)
    for h in range(unique // 256):
        out_ref[:, h * 256:(h + 1) * 256] = acc[h * c:(h + 1) * c].astype(BF)


def owner_pick(asked_ref, enc_ref, out_ref):
    c, unique = enc_ref.shape
    reps, cap = asked_ref.shape
    enc = enc_ref[...]
    tall = jnp.concatenate([enc[:, h * 256:(h + 1) * 256] for h in range(unique // 256)], axis=0)
    for r in range(reps):
        asked = asked_ref[r:r + 1, :]
        got = nn(tall, one_hot(asked & 255, 256))
        out = jnp.zeros((c, cap), F32)
        for h in range(unique // 256):
            out = jnp.where((asked >> 8) == h, got[h * c:(h + 1) * c], out)
        out_ref[r * c:(r + 1) * c, :] = out.astype(BF)


def local(body, shape, scratch, *args):
    return pl.pallas_call(
        body, in_specs=[VM] * len(args), out_specs=VM,
        out_shape=jax.ShapeDtypeStruct(shape, BF), scratch_shapes=scratch,
        compiler_params=pltpu.CompilerParams(vmem_limit_bytes=48 << 20),
    )(*args)


MESH = pl.DeviceIdType.MESH


def send(src, dst, ssem, rsem, **to):
    return pltpu.make_async_remote_copy(
        src_ref=src, dst_ref=dst, send_sem=ssem, recv_sem=rsem, device_id=to, device_id_type=MESH)


def rows_at(ref, start, count):
    return ref.at[pl.ds(pl.multiple_of(start, count), count)]


class Place:
    def __init__(self):
        e = lax.axis_index("enc")
        self.chips = lax.axis_size("enc") // 2
        self.y, self.k = e // 2, lax.rem(e, 2)
        self.sib = self.y * 2 + 1 - self.k
        self.right = self.at(1)
        self.left = self.at(-1)

    def at(self, d, other=False):
        yy = lax.rem(self.y + d + self.chips, self.chips)
        return yy * 2 + (1 - self.k if other else self.k)


class Gather:
    def __init__(self, place, whole, rows, ssem, rsem, index):
        self.p, self.whole, self.rows = place, whole, rows
        self.s = lambda i: ssem.at[index, i]
        self.r = lambda i: rsem.at[index, i]

    def half(self, e, which):
        h = self.rows // 2
        return rows_at(self.whole, e * self.rows + which * h, h)

    def copy(self, i, ref, to):
        return send(ref, ref, self.s(i), self.r(i), enc=to)

    def start(self):
        p = self.p
        own = p.at(0)
        self.sends = [
            self.copy(0, self.half(own, 0), p.right),
            self.copy(1, self.half(own, 1), p.left),
            self.copy(2, self.half(own, 1), p.right),
            self.copy(3, self.half(own, 0), p.left),
            self.copy(4, rows_at(self.whole, own * self.rows, self.rows), p.sib),
        ]
        for c in self.sends:
            c.start()

    def more(self, i, ref, to):
        c = self.copy(i, ref, to)
        c.start()
        self.sends.append(c)

    def arrived(self, i, ref):
        self.copy(i, ref, self.p.sib).wait_recv()

    def forward1(self):
        p = self.p
        la, rb = self.half(p.at(-1), 0), self.half(p.at(1), 1)
        self.arrived(0, la)
        self.more(5, la, p.right)
        self.arrived(1, rb)
        self.more(6, rb, p.left)
        self.more(7, la, p.sib)
        self.more(8, rb, p.sib)

    def forward2(self):
        p = self.p
        lb, ra = self.half(p.at(-1), 1), self.half(p.at(1), 0)
        self.arrived(2, lb)
        self.more(9, lb, p.sib)
        self.arrived(3, ra)
        self.more(10, ra, p.sib)

    def wait_sib(self):
        self.arrived(4, rows_at(self.whole, self.p.sib * self.rows, self.rows))

    def forward3(self):
        p = self.p
        oa, ob = self.half(p.at(2), 0), self.half(p.at(2), 1)
        self.arrived(5, oa)
        self.more(11, oa, p.sib)
        self.arrived(6, ob)
        self.more(12, ob, p.sib)

    def finish_near(self):
        p = self.p
        for i, d, h in ((7, -1, 0), (8, 1, 1), (9, -1, 1), (10, 1, 0)):
            self.arrived(i, self.half(p.at(d, True), h))

    def finish_far(self):
        p = self.p
        for i, h in ((11, 0), (12, 1)):
            self.arrived(i, self.half(p.at(2, True), h))

    def drain(self):
        for c in self.sends:
            c.wait_send()


class Scatter:
    def __init__(self, place, rows, bufs, ssem, rsem, index):
        self.p, self.rows = place, rows
        self.sib_out, self.sib_in, self.ring, self.xin, self.lin, self.rin, self.own = bufs
        self.s = lambda i: ssem.at[index, i]
        self.r = lambda i: rsem.at[index, i]
        self.sends = []

    def go(self, i, src, dst, to):
        c = send(src, dst, self.s(i), self.r(i), enc=to)
        c.start()
        self.sends.append(c)

    def arrived(self, i, dst):
        send(dst, dst, self.s(i), self.r(i), enc=self.p.sib).wait_recv()

    def block(self, ref, d, which=None):
        if which is None:
            return ref.at[d * self.rows:(d + 1) * self.rows]
        h = self.rows // 2
        return ref.at[d * self.rows + which * h:d * self.rows + (which + 1) * h]

    def start(self, compute):
        p = self.p
        for d in (2, 1, 3, 0):
            self.block(self.sib_out, d)[...] = compute(p.at(d, True)).astype(BF)
            self.go(d, self.block(self.sib_out, d), self.block(self.sib_in, d), p.sib)
        for d in (2, 1, 3, 0):
            mine = compute(p.at(d))
            other = self.block(self.sib_in, d)
            self.arrived(d, other)
            mine = mine + other[...].astype(F32)
            if d == 0:
                self.own[...] = mine
                continue
            self.block(self.ring, d)[...] = mine.astype(BF)
            if d == 2:
                self.go(4, self.block(self.ring, 2, 0), self.block(self.xin, 0, 0), p.right)
                self.go(5, self.block(self.ring, 2, 1), self.block(self.xin, 0, 1), p.left)
            if d == 1:
                self.go(6, self.block(self.ring, 1, 1), self.block(self.lin, 0, 1), p.right)
            if d == 3:
                self.go(7, self.block(self.ring, 3, 0), self.block(self.rin, 0, 0), p.left)

    def mid(self):
        p = self.p
        for i, d, h, dst, to in ((4, 1, 0, self.lin, p.right), (5, 3, 1, self.rin, p.left)):
            came, mine = self.block(self.xin, 0, h), self.block(self.ring, d, h)
            self.arrived(i, came)
            mine[...] = (mine[...].astype(F32) + came[...].astype(F32)).astype(BF)
            self.go(i + 4, mine, self.block(dst, 0, h), to)

    def finish(self):
        self.arrived(6, self.block(self.lin, 0, 1))
        self.arrived(7, self.block(self.rin, 0, 0))
        self.arrived(8, self.block(self.lin, 0, 0))
        self.arrived(9, self.block(self.rin, 0, 1))

    def drain(self):
        for c in self.sends:
            c.wait_send()


class Ring:
    def __init__(self, block, half, bufs, plus, minus, ssem, rsem, index):
        self.block, self.half, self.plus, self.minus = block, half, plus, minus
        self.xin, self.lin, self.rin = bufs
        self.s = lambda i: ssem.at[index, i]
        self.r = lambda i: rsem.at[index, i]
        self.sends = []

    def go(self, i, src, dst, to):
        c = send(src, dst, self.s(i), self.r(i), dp=to)
        c.start()
        self.sends.append(c)

    def arrived(self, i, dst):
        send(dst, dst, self.s(i), self.r(i), dp=self.plus).wait_recv()

    def start(self):
        self.go(0, self.block(2, 0), self.half(self.xin, 0), self.plus)
        self.go(1, self.block(2, 1), self.half(self.xin, 1), self.minus)
        self.go(2, self.block(1, 1), self.half(self.lin, 1), self.plus)
        self.go(3, self.block(3, 0), self.half(self.rin, 0), self.minus)

    def mid(self):
        for i, d, h, dst, to in ((0, 1, 0, self.lin, self.plus), (1, 3, 1, self.rin, self.minus)):
            came, mine = self.half(self.xin, h), self.block(d, h)
            self.arrived(i, came)
            mine[...] = (mine[...].astype(F32) + came[...].astype(F32)).astype(BF)
            self.go(4 + i, mine, self.half(dst, h), to)

    def finish(self):
        self.arrived(2, self.half(self.lin, 1))
        self.arrived(3, self.half(self.rin, 0))
        self.arrived(4, self.half(self.lin, 0))
        self.arrived(5, self.half(self.rin, 1))

    def drain(self):
        for c in self.sends:
            c.wait_send()


class Plane:
    def __init__(self, out, bufs, ssem, rsem, index):
        n = lax.axis_size("dp")
        side = math.isqrt(n)
        me = lax.axis_index("dp")
        z, x = me // side, lax.rem(me, side)
        self.out, self.z, self.x = out, z, x
        rows, cols = out.shape[2], out.shape[3] // 2
        self.cols = cols

        def step_x(d):
            return lax.rem(x + d, side)

        def step_z(d):
            return lax.rem(z + d, side)

        along_x = (z * side + step_x(1), z * side + step_x(side - 1))
        along_z = (step_z(1) * side + x, step_z(side - 1) * side + x)
        two = lambda h: slice(2 * h, 2 * h + 2)
        part = lambda h: slice(h * rows // 2, (h + 1) * rows // 2)
        first, second, self.mids = bufs[0:6], bufs[6:12], bufs[12:14]
        half1 = lambda ref, h: ref.at[two(h)]
        half2 = lambda ref, h: ref.at[part(h)]
        self.first = [
            Ring(lambda d, h: out.at[two(h), step_x(d), :, :cols], half1, first[:3], *along_x,
                 ssem, rsem, index),
            Ring(lambda d, h: out.at[step_z(d), two(h), :, cols:], half1, first[3:], *along_z,
                 ssem, rsem, index + 1),
        ]
        self.second = [
            Ring(lambda d, h: self.mids[0].at[step_z(d), part(h)], half2, second[:3], *along_z,
                 ssem, rsem, index + 2),
            Ring(lambda d, h: self.mids[1].at[step_x(d), part(h)], half2, second[3:], *along_x,
                 ssem, rsem, index + 3),
        ]

    def start(self):
        for ring in self.first:
            ring.start()

    def mid(self):
        for ring in self.first:
            ring.mid()

    def turn(self):
        for i, ring in enumerate(self.first):
            ring.finish()
            own = (self.out[:, self.x, :, :self.cols] if i == 0
                   else self.out[self.z, :, :, self.cols:])
            self.mids[i][...] = (own.astype(F32) + ring.lin[...].astype(F32)
                                 + ring.rin[...].astype(F32)).astype(BF)
        for ring in self.second:
            ring.start()

    def mid2(self):
        for ring in self.second:
            ring.mid()

    def finish(self):
        got = []
        for i, ring in enumerate(self.second):
            ring.finish()
            own = self.mids[i][self.z if i == 0 else self.x]
            got.append(own.astype(F32) + ring.lin[...].astype(F32) + ring.rin[...].astype(F32))
        return got

    def drain(self):
        for ring in self.first + self.second:
            ring.drain()


def plane_bufs(side, rows, cols):
    return [((side, rows, cols), BF)] * 6 + [((rows, cols), BF)] * 6 + [((side, rows, cols), BF)] * 2


def scatter_bufs(rows, n):
    return [((4 * rows, n), BF)] * 3 + [((rows, n), BF)] * 3 + [((rows, n), F32)]


class Exchange:
    def __init__(self, src, dst, rows, ssem, rsem, index):
        self.src, self.dst, self.rows = src, dst, rows
        self.n = lax.axis_size("dp")
        self.me = lax.axis_index("dp")
        self.ssem, self.rsem, self.index = ssem, rsem, index

    def at(self, ref, i):
        return ref.at[i] if self.rows is None else rows_at(ref, i * self.rows, self.rows)

    def copy(self, j):
        to = lax.rem(self.me + j, self.n)
        return send(self.at(self.src, to), self.at(self.dst, self.me),
                    self.ssem.at[self.index, j], self.rsem.at[self.index, j], dp=to)

    def start(self):
        def body(j, carry):
            self.copy(j).start()
            return carry
        lax.fori_loop(1, self.n, body, 0)
        self.at(self.dst, self.me)[...] = self.at(self.src, self.me)[...]

    def wait(self):
        def body(j, carry):
            came = self.at(self.dst, lax.rem(self.me - j + self.n, self.n))
            send(came, came, self.ssem.at[self.index, j], self.rsem.at[self.index, j],
                 dp=lax.rem(self.me + 1, self.n)).wait_recv()
            return carry
        lax.fori_loop(1, self.n, body, 0)

    def drain(self):
        def body(j, carry):
            self.copy(j).wait_send()
            return carry
        lax.fori_loop(1, self.n, body, 0)


def chunks(count, step, body):
    def run(i, carry):
        body(pl.ds(pl.multiple_of(i * step, step), step), i * step)
        return carry
    lax.fori_loop(0, count // step, run, 0)


INPUTS = ("features", "weight_in", "bias", "proj", "pbias", "slot", "d_tokens", "requests")
OUTPUTS = ("tokens", "d_features", "d_high", "d_proj")


def step_kernel(names, *refs):
    r = dict(zip(INPUTS + OUTPUTS + names, refs))
    place = Place()
    n_dp, me = lax.axis_size("dp"), lax.axis_index("dp")
    filters, words = r["features"].shape
    total = r["whole0"].shape[0]
    c, tokens = r["d_tokens"].shape
    cap = r["requests"].shape[1]
    e = place.at(0)
    raw = pltpu.make_async_copy(r["weight_in"].at[0], r["raw"], r["raw_s"].at[0])
    raw.start()
    for o in range(n_dp):
        r["wanted"][o] = r["requests"][o:o + 1, :]

    barrier = pltpu.get_barrier_semaphore()
    for to in (place.left, place.right, place.sib):
        pl.semaphore_signal(barrier, inc=1, device_id={"enc": to}, device_id_type=MESH)

    def greet(j, carry):
        pl.semaphore_signal(barrier, inc=1, device_id={"dp": lax.rem(me + j, n_dp)},
                            device_id_type=MESH)
        return carry
    lax.fori_loop(1, n_dp, greet, 0)

    own_rows = pl.ds(pl.multiple_of(e * filters, filters), filters)
    r["whole0"][own_rows, :] = r["features"][...]
    pl.semaphore_wait(barrier, 3 + n_dp - 1)

    gather = [Gather(place, r["whole0"], filters, r["ag_s"], r["ag_r"], 0),
              Gather(place, r["whole1"], filters, r["ag_s"], r["ag_r"], 1),
              Gather(place, r["grads"], c, r["ag_s"], r["ag_r"], 2)]
    sums = [Scatter(place, filters, [r[f"rs{0 if j in (0, 2) else i}_{j}"] for j in range(7)], r["rs_s"], r["rs_r"], i)
            for i in range(2)]
    proj_sum = Scatter(place, c, [r[f"rs2_{j}"] for j in range(7)], r["rs_s"], r["rs_r"], 2)
    high_rows = total // n_dp
    proj_rows = r["proj"].shape[1] // n_dp

    def exchange(src, dst, rows, index):
        return Exchange(r[src], r[dst], rows, r["dp_s"], r["dp_r"], index)

    asked = exchange("wanted", "asked", None, 0)
    slots = exchange("slot_out", "slot_in", c, 1)
    picked = exchange("pick_out", "pick_in", c, 2)
    d_proj = exchange("dp_out", "dp_in", proj_rows, 3)
    d_high = [Plane(r[f"dh{l}_out"], [r[f"dh{l}_{j}"] for j in range(14)], r["ring_s"], r["ring_r"], 4 * l)
              for l in range(2)]

    gather[0].start()
    asked.start()

    def unpack(l):
        raw.wait()

        def body(at, start):
            r["weight"][l, at, :] = r["raw"][at].reshape(64, 2 * filters)
        chunks(total, 64, body)

    unpack(0)
    raw = pltpu.make_async_copy(r["weight_in"].at[1], r["raw"], r["raw_s"].at[1])
    raw.start()

    def layer(l, gat, whole, before, between, next_ref):
        acc, weight = r["acc"], r["weight"]

        def add(block, first=False):
            at = pl.ds(pl.multiple_of(block * filters, filters), filters)
            part = tn(weight[l, at, :], whole[at, :])
            acc[...] = part if first else acc[...] + part

        if l == 1:
            unpack(1)
        add(e, True)
        if before is not None:
            before()
        gat.forward1()
        between()
        gat.wait_sib()
        add(place.sib)
        gat.forward2()

        def near(i, carry):
            add(place.at(2 * i - 1))
            return carry
        lax.fori_loop(0, 2, near, 0)
        gat.forward3()
        add(place.at(2))
        gat.finish_near()

        def near_other(i, carry):
            add(place.at(2 * i - 1, True))
            return carry
        lax.fori_loop(0, 2, near_other, 0)
        gat.finish_far()
        add(place.at(2, True))
        for i in range(2):
            r["bcol"][i * filters:(i + 1) * filters, :] = jnp.broadcast_to(
                r["bias"][l, i:i + 1, :], (128, filters)).T

        def mix(at, start):
            low = pl.ds(pl.multiple_of(filters + start, 32), 32)
            t = acc[at, :] + jnp.tile(r["bcol"][at, :], (1, words // 128))
            g = jax.nn.sigmoid(acc[low, :] + jnp.tile(r["bcol"][low, :], (1, words // 128)))
            r["t"][l, at, :] = t
            r["g"][l, at, :] = g
            h = whole[pl.ds(pl.multiple_of(e * filters + start, 32), 32), :].astype(F32)
            out = (g * (t * jax.nn.sigmoid(t)) + (1.0 - g) * h).astype(BF)
            if next_ref is r["top"]:
                next_ref[at, :] = out
            else:
                next_ref[pl.ds(pl.multiple_of(e * filters + start, 32), 32), :] = out
        chunks(filters, 32, mix)
        gat.drain()

    n_chunks = tokens // 1024
    r["sacc"][...] = jnp.zeros_like(r["sacc"])

    def slot_part(first, last):
        def body(i, carry):
            at = pl.ds(pl.multiple_of(i * 1024, 1024), 1024)
            slot = r["slot"][:, at]
            hot = one_hot(slot & 255, 256)
            high = slot >> 8
            d = r["d_tokens"][:, at]
            parts = [d * jnp.where(high == o, 1.0, 0.0).astype(BF) for o in range(n_dp)]
            r["sacc"][...] += nt(jnp.concatenate(parts, axis=0), hot)
            return carry
        lax.fori_loop(first, last, body, 0)

    def slot_rest():
        slot_part(n_chunks // 2, n_chunks)
        r["slot_out"][...] = r["sacc"][...].astype(BF)
        slots.start()

    layer(0, gather[0], r["whole0"], lambda: slot_part(0, n_chunks // 2), slot_rest, r["whole1"])
    gather[1].start()
    asked.wait()
    for o in range(n_dp):
        r["asked2"][o:o + 1, :] = r["asked"][o]

    def owner_part():
        slots.wait()
        owner_sums(r["asked2"], r["slot_in"], r["row"])
        r["grads"][pl.ds(pl.multiple_of(e * c, c), c), :] = r["row"][...]
        gather[2].start()

    layer(1, gather[1], r["whole1"], None, owner_part, r["top"])

    top, proj = r["top"], r["proj"]
    width = r["proj"].shape[1]
    r["acc"][...] = tn(proj[...], top[...])
    proj_sum.start(lambda dest: r["acc"][pl.ds(pl.multiple_of(dest * c, c), c), :])
    gather[2].forward1()
    gather[2].forward2()
    gather[2].forward3()
    gather[2].wait_sib()
    gather[2].finish_near()
    gather[2].finish_far()
    up = r["up"]
    up[...] = nn(proj[...], r["grads"][...])
    proj_sum.mid()

    def cell(l):
        whole = r[f"whole{l}"]

        def body(at, start):
            t, g, u = r["t"][l, at, :], r["g"][l, at, :], up[at, :]
            h = whole[pl.ds(pl.multiple_of(e * filters + start, 32), 32), :].astype(F32)
            s = jax.nn.sigmoid(t)
            r["pre"][l, at, :] = (u * g * (s * (1.0 + t * (1.0 - s)))).astype(BF)
            low = pl.ds(pl.multiple_of(filters + start, 32), 32)
            r["pre"][l, low, :] = (u * (t * s - h) * g * (1.0 - g)).astype(BF)
            up[at, :] = u * (1.0 - g)
        chunks(filters, 32, body)

    def back(l):
        return lambda dest: nn(
            r["weight"][l, pl.ds(pl.multiple_of(dest * filters, filters), filters), :], r["pre"][l])

    def high_term(l):
        out = r[f"dh{l}_out"]
        side = out.shape[0]

        def body(z, carry):
            for x in range(0, side, 2):
                at = pl.ds(pl.multiple_of((z * side + x) * high_rows, 2 * high_rows), 2 * high_rows)
                got = nt(r[f"whole{l}"][at, :], r["pre"][l]).astype(BF)
                out[z, x:x + 2] = got.reshape(2, high_rows, 2 * filters)
            return carry
        lax.fori_loop(0, side, body, 0)
        d_high[l].start()

    def add_up(l, last):
        s = sums[l]

        def body(at, start):
            new = up[at, :] + (s.own[at, :] + s.lin[at, :].astype(F32) + s.rin[at, :].astype(F32))
            up[at, :] = new
        chunks(filters, 32, body)

    def high_sum(l):
        for i, got in enumerate(d_high[l].finish()):
            r["d_high"][l, :, i, :] = got

    cell(1)
    sums[1].start(back(1))
    proj_sum.finish()
    r["encoded"][...] = (
        proj_sum.own[...] + proj_sum.lin[...].astype(F32) + proj_sum.rin[...].astype(F32)
        + column(jnp.concatenate([r["pbias"][...], jnp.zeros((1, 128 - c), F32)], axis=1))[:c]).astype(BF)
    owner_pick(r["asked2"], r["encoded"], r["pick_out"])
    picked.start()
    high_term(1)
    sums[1].mid()
    d_high[1].mid()
    r["dp_out"][...] = nt(r["grads"][...], top[...]).astype(BF)
    d_proj.start()
    d_high[1].turn()
    sums[1].finish()
    add_up(1, False)
    cell(0)
    sums[1].drain()
    high_term(0)
    sums[0].start(back(0))
    d_high[1].mid2()
    d_high[0].mid()
    sums[0].mid()
    picked.wait()
    token_pick(r["slot"], r["pick_in"], r["tokens"])
    high_sum(1)
    d_high[0].turn()
    d_proj.wait()
    got = jnp.zeros((proj_rows, filters), F32)
    for i in range(n_dp):
        got = got + r["dp_in"][i * proj_rows:(i + 1) * proj_rows, :].astype(F32)
    r["d_proj"][...] = got
    d_high[0].mid2()
    sums[0].finish()
    add_up(0, True)
    r["d_features"][...] = up[...].T.astype(BF)
    high_sum(0)
    for x in (asked, slots, picked, d_proj, d_high[0], d_high[1], gather[2], sums[0], proj_sum):
        x.drain()


def step(features, weight, bias, proj, pbias, slot, d_tokens, requests, n_dp):
    filters, words = features.shape
    total = weight.shape[1]
    c, tokens = d_tokens.shape
    width = proj.shape[1]
    cap = requests.shape[1]
    bufs = {
        "whole0": ((total, words), BF), "whole1": ((total, words), BF), "grads": ((width, words), BF),
        "top": ((filters, words), BF), "acc": ((2 * filters, words), F32),
        "bcol": ((2 * filters, 128), F32),
        "t": ((2, filters, words), F32), "g": ((2, filters, words), F32),
        "pre": ((2, 2 * filters, words), BF), "up": ((filters, words), F32),
        "sacc": ((n_dp * c, cap), F32),
        "slot_out": ((n_dp * c, cap), BF), "slot_in": ((n_dp * c, cap), BF),
        "pick_out": ((n_dp * c, cap), BF), "pick_in": ((n_dp * c, cap), BF),
        "row": ((c, words), BF), "encoded": ((c, words), BF),
        "dp_out": ((width, filters), BF), "dp_in": ((width, filters), BF),
        "weight": ((2, total, 2 * filters), BF), "raw": ((total, 2, filters), BF),
        "wanted": ((n_dp, 1, cap), jnp.int32), "asked": ((n_dp, 1, cap), jnp.int32), "asked2": ((n_dp, cap), jnp.int32),
    }
    for l in range(2):
        side = math.isqrt(n_dp)
        bufs[f"dh{l}_out"] = ((side, side, total // n_dp, 2 * filters), BF)
        for j, spec in enumerate(plane_bufs(side, total // n_dp, filters)):
            bufs[f"dh{l}_{j}"] = spec
    for i, rows in enumerate((filters, filters, c)):
        for j, spec in enumerate(scatter_bufs(rows, words)):
            if i != 1 or j not in (0, 2):
                bufs[f"rs{i}_{j}"] = spec
    scratch = [pltpu.VMEM(*spec) for spec in bufs.values()]
    sems = {"ag": (3, 13), "rs": (3, 10), "dp": (4, n_dp), "ring": (8, 6), "raw": (2,)}
    names = tuple(bufs)
    for name, dims in sems.items():
        names += (name + "_s", name + "_r")
        scratch += [pltpu.SemaphoreType.DMA(dims)] * 2
    return pl.pallas_call(
        functools.partial(step_kernel, names),
        in_specs=[pl.BlockSpec(memory_space=pl.ANY) if x == "weight_in" else VM for x in INPUTS], out_specs=[VM] * len(OUTPUTS),
        out_shape=[
            jax.ShapeDtypeStruct((c, tokens), BF),
            jax.ShapeDtypeStruct((words, filters), BF),
            jax.ShapeDtypeStruct((2, total // n_dp, 2, filters), F32),
            jax.ShapeDtypeStruct((width // n_dp, filters), F32),
        ],
        scratch_shapes=scratch,
        compiler_params=pltpu.CompilerParams(
            collective_id=0, has_side_effects=True, vmem_limit_bytes=62 << 20),
    )(features, weight, bias, proj, pbias, slot, d_tokens, requests)


def hand_on(*arrays):
    n = len(arrays)

    def kernel(*refs):
        for i in range(n):
            refs[n + i][...] = refs[i][...]

    return pl.pallas_call(
        kernel, in_specs=[VM] * n, out_specs=[VM] * n,
        out_shape=[jax.ShapeDtypeStruct(a.shape, a.dtype) for a in arrays],
        compiler_params=pltpu.CompilerParams(vmem_limit_bytes=63 << 20),
    )(*arrays)


def per_device(chars, char_table, conv_weight, conv_bias, hw_weight, hw_bias, proj_weight,
               proj_bias, owner_types, requests, tok_slot, d_tokens):
    taps, embed_width, filters = conv_weight.shape
    layers, total = hw_weight.shape[:2]
    unique = owner_types.shape[0]
    owners, cap = requests.shape[1:]
    tokens, c = d_tokens.shape
    features = encode(chars.T, owner_types.reshape(1, unique), char_table.T,
                      conv_weight.reshape(taps * embed_width, filters),
                      conv_bias.reshape(1, filters), total)
    outs = step(
        features, hw_weight, hw_bias, proj_weight, proj_bias.reshape(1, c),
        tok_slot.reshape(1, tokens), d_tokens.T, requests.reshape(owners, cap), owners)
    tok, d_feat, d_high, d_proj = hand_on(*outs)
    return tok.T, d_feat, d_high, d_proj.T


def solution(mesh):
    return jax.shard_map(
        per_device,
        mesh=mesh,
        in_specs=(
            P("dp", None), P(), P(None, None, "enc"), P("enc"), P(None, None, None, "enc"),
            P(None, None, "enc"), P("enc", None), P("enc"), P("dp"), P("dp", None, None),
            P("dp"), P("dp", "enc"),
        ),
        out_specs=(P("dp", "enc"), P("dp", "enc"), P(None, "dp", None, "enc"), P("enc", "dp")),
        check_vma=False,
    )
```

```python
import math
import functools
import jax
import jax.numpy as jnp
from jax import lax
from jax.experimental import pallas as pl
from jax.experimental.pallas import tpu as pltpu
from jax.sharding import PartitionSpec as P

BF = jnp.bfloat16
F32 = jnp.float32
VM = pl.BlockSpec(memory_space=pltpu.VMEM)
BASE = 128


def width_of(index, total):
    width = jnp.ones(index.shape, jnp.int32)
    for share in (1, 2, 4, 8, 16, 32):
        width = width + (index >= share * total // 64).astype(jnp.int32)
    return width


def one_hot(row, count):
    n = row.shape[1]
    return jnp.where(
        lax.broadcasted_iota(jnp.int32, (count, n), 0) == row, 1.0, 0.0
    ).astype(BF)


def nt(a, b):
    return lax.dot_general(a, b, (((1,), (1,)), ((), ())), preferred_element_type=F32)


def nn(a, b):
    return jnp.dot(a, b, preferred_element_type=F32)


def tn(a, b):
    return lax.dot_general(a, b, (((0,), (0,)), ((), ())), preferred_element_type=F32)


def column(row):
    return jnp.broadcast_to(row, (128, row.shape[1])).T[:, :1]


def encode_kernel(total, length, chars_ref, types_ref, letters_ref, weight_ref, bias_ref,
                  out_ref, hot, lhs, acc, vec, band, best, table_ref):
    step = pl.program_id(0)
    words = types_ref.shape[1]
    lanes = 256
    group = chars_ref.shape[1] // lanes
    rows = 64

    @pl.when(step == 0)
    def _():
        hot[...] = one_hot(types_ref[...] & (lanes - 1), lanes)
        acc[...] = jnp.zeros_like(acc)
        lhs[...] = jnp.zeros_like(lhs)
        table_ref[...] = jnp.zeros_like(table_ref)
        table_ref[:, :letters_ref.shape[1]] = letters_ref[...].astype(F32)

    high = types_ref[...] // lanes
    for part in range(group // 8):
        for j in range(8):
            block = chars_ref[:, (part * 8 + j) * lanes:(part * 8 + j + 1) * lanes]
            lhs[j * rows:j * rows + length, :] = (block - BASE).astype(F32).astype(BF)
        for half in range(words // 256):
            cols = slice(half * 256, half * 256 + 256)
            picked = nn(lhs[...], hot[:, cols])
            here = acc[:, cols]
            for j in range(8):
                here = jnp.where(high[:, cols] == step * group + part * 8 + j,
                                 picked[j * rows:(j + 1) * rows], here)
            acc[:, cols] = here

    @pl.when(step == pl.num_programs(0) - 1)
    def _():
        filters = weight_ref.shape[1]
        vec[length * 16:, :] = jnp.zeros((vec.shape[0] - length * 16, words), BF)

        def embed(p, carry):
            row = acc[pl.ds(p, 1), :].astype(jnp.int32) + BASE
            for b in range(words // 128):
                idx = jnp.broadcast_to(row[:, b * 128:(b + 1) * 128], (8, 128))
                low, seg = idx & 127, idx >> 7
                halves = []
                for h in range(2):
                    got = None
                    for s in range(3):
                        tab = table_ref[h * 8:(h + 1) * 8, s * 128:(s + 1) * 128]
                        val = jnp.take_along_axis(tab, low, axis=1)
                        got = val if got is None else jnp.where(seg == s, val, got)
                    halves.append(got)
                vec[pl.ds(pl.multiple_of(p * 16, 16), 16), b * 128:(b + 1) * 128] = (
                    jnp.concatenate(halves, axis=0).astype(BF))
            return carry

        lax.fori_loop(0, length, embed, 0, unroll=5)

        base = lax.axis_index("enc") * filters
        width_row = width_of(base + lax.broadcasted_iota(jnp.int32, (128, filters), 1), total)
        tap = lax.broadcasted_iota(jnp.int32, (128, filters), 0) // 16
        raw = jnp.concatenate(
            [weight_ref[...].astype(F32), jnp.zeros((128 - weight_ref.shape[0], filters), F32)],
            axis=0)
        kt = jnp.where(tap < width_row, raw, 0.0).T
        wide = jnp.concatenate([kt, jnp.zeros((filters, 128), F32)], axis=1)
        for q in range(8):
            moved = wide if q == 0 else pltpu.roll(wide, q * 16, 1)
            band[q * filters:(q + 1) * filters, :] = moved.astype(BF)
        best[...] = jnp.full(best.shape, -jnp.inf, F32)
        width_col = width_of(base + lax.broadcasted_iota(jnp.int32, (filters, 256), 0), total)
        groups = -(-length // 8)

        def conv(g, first, count, masked):
            for half in range(words // 256):
                cols = slice(half * 256, half * 256 + 256)
                win = vec[pl.ds(pl.multiple_of(g * 128, 128), 256), cols]
                out = nn(band[:count * filters, :], win)
                m = best[:, cols]
                for q in range(count):
                    val = out[q * filters:(q + 1) * filters]
                    if masked and first + q + 7 > length:
                        val = jnp.where(width_col <= length - first - q, val, -jnp.inf)
                    m = jnp.maximum(m, val)
                best[:, cols] = m

        def body(g, carry):
            conv(g, 0, 8, False)
            return carry

        lax.fori_loop(0, groups - 2, body, 0)
        for g in (groups - 2, groups - 1):
            conv(g, g * 8, min(8, length - g * 8), True)
        out_ref[...] = jnp.maximum(best[...] + column(bias_ref[...]), 0.0).astype(BF)


def encode(chars_t, types, table_t, weight, bias, total):
    length, count = chars_t.shape
    words = types.shape[1]
    filters = weight.shape[1]
    block = 8192
    return pl.pallas_call(
        functools.partial(encode_kernel, total, length),
        grid=(count // block,),
        in_specs=[pl.BlockSpec((length, block), lambda i: (0, i)), VM, VM, VM, VM],
        out_specs=VM,
        out_shape=jax.ShapeDtypeStruct((filters, words), BF),
        scratch_shapes=[
            pltpu.VMEM((256, words), BF),
            pltpu.VMEM((512, 256), BF),
            pltpu.VMEM((64, words), F32),
            pltpu.VMEM((1024, words), BF),
            pltpu.VMEM((8 * filters, 256), BF),
            pltpu.VMEM((filters, words), F32),
            pltpu.VMEM((16, 384), F32),
        ],
        compiler_params=pltpu.CompilerParams(vmem_limit_bytes=63 << 20),
    )(chars_t, types, table_t, weight, bias)


def slot_sums(slot_ref, d_ref, out_ref, acc, chunk=1024):
    c, tokens = d_ref.shape
    owners = out_ref.shape[0] // c
    acc[...] = jnp.zeros_like(acc)

    def body(i, carry):
        at = pl.ds(pl.multiple_of(i * chunk, chunk), chunk)
        slot = slot_ref[:, at]
        hot = one_hot(slot & 255, 256)
        high = slot >> 8
        d = d_ref[:, at]
        parts = [d * jnp.where(high == o, 1.0, 0.0).astype(BF) for o in range(owners)]
        acc[...] += nt(jnp.concatenate(parts, axis=0), hot)
        return carry

    lax.fori_loop(0, tokens // chunk, body, 0)
    out_ref[...] = acc[...].astype(BF)


def token_pick(slot_ref, ret_ref, out_ref, chunk=1024):
    c, tokens = out_ref.shape
    owners = ret_ref.shape[0] // c

    def body(i, carry):
        at = pl.ds(pl.multiple_of(i * chunk, chunk), chunk)
        slot = slot_ref[:, at]
        got = nn(ret_ref[...], one_hot(slot & 255, 256))
        high = slot >> 8
        out = jnp.zeros((c, chunk), F32)
        for o in range(owners):
            out = jnp.where(high == o, got[o * c:(o + 1) * c], out)
        out_ref[:, at] = out.astype(BF)
        return carry

    lax.fori_loop(0, tokens // chunk, body, 0)


def owner_sums(asked_ref, arr_ref, out_ref):
    c, unique = out_ref.shape
    reps, cap = asked_ref.shape
    acc = jnp.zeros((unique // 256 * c, 256), F32)
    for r in range(reps):
        asked = asked_ref[r:r + 1, :]
        hot = one_hot(asked & 255, 256)
        a = arr_ref[r * c:(r + 1) * c, :]
        parts = [a * jnp.where((asked >> 8) == h, 1.0, 0.0).astype(BF) for h in range(unique // 256)]
        acc += nt(jnp.concatenate(parts, axis=0), hot)
    for h in range(unique // 256):
        out_ref[:, h * 256:(h + 1) * 256] = acc[h * c:(h + 1) * c].astype(BF)


def owner_pick(asked_ref, enc_ref, out_ref):
    c, unique = enc_ref.shape
    reps, cap = asked_ref.shape
    enc = enc_ref[...]
    tall = jnp.concatenate([enc[:, h * 256:(h + 1) * 256] for h in range(unique // 256)], axis=0)
    for r in range(reps):
        asked = asked_ref[r:r + 1, :]
        got = nn(tall, one_hot(asked & 255, 256))
        out = jnp.zeros((c, cap), F32)
        for h in range(unique // 256):
            out = jnp.where((asked >> 8) == h, got[h * c:(h + 1) * c], out)
        out_ref[r * c:(r + 1) * c, :] = out.astype(BF)


def local(body, shape, scratch, *args):
    return pl.pallas_call(
        body, in_specs=[VM] * len(args), out_specs=VM,
        out_shape=jax.ShapeDtypeStruct(shape, BF), scratch_shapes=scratch,
        compiler_params=pltpu.CompilerParams(vmem_limit_bytes=48 << 20),
    )(*args)


MESH = pl.DeviceIdType.MESH


def send(src, dst, ssem, rsem, **to):
    return pltpu.make_async_remote_copy(
        src_ref=src, dst_ref=dst, send_sem=ssem, recv_sem=rsem, device_id=to, device_id_type=MESH)


def rows_at(ref, start, count):
    return ref.at[pl.ds(pl.multiple_of(start, count), count)]


class Place:
    def __init__(self):
        e = lax.axis_index("enc")
        self.chips = lax.axis_size("enc") // 2
        self.y, self.k = e // 2, lax.rem(e, 2)
        self.sib = self.y * 2 + 1 - self.k
        self.right = self.at(1)
        self.left = self.at(-1)

    def at(self, d, other=False):
        yy = lax.rem(self.y + d + self.chips, self.chips)
        return yy * 2 + (1 - self.k if other else self.k)


class Gather:
    def __init__(self, place, whole, rows, ssem, rsem, index):
        self.p, self.whole, self.rows = place, whole, rows
        self.s = lambda i: ssem.at[index, i]
        self.r = lambda i: rsem.at[index, i]

    def half(self, e, which):
        h = self.rows // 2
        return rows_at(self.whole, e * self.rows + which * h, h)

    def copy(self, i, ref, to):
        return send(ref, ref, self.s(i), self.r(i), enc=to)

    def start(self):
        p = self.p
        own = p.at(0)
        self.sends = [
            self.copy(0, self.half(own, 0), p.right),
            self.copy(1, self.half(own, 1), p.left),
            self.copy(2, self.half(own, 1), p.right),
            self.copy(3, self.half(own, 0), p.left),
            self.copy(4, rows_at(self.whole, own * self.rows, self.rows), p.sib),
        ]
        for c in self.sends:
            c.start()

    def more(self, i, ref, to):
        c = self.copy(i, ref, to)
        c.start()
        self.sends.append(c)

    def arrived(self, i, ref):
        self.copy(i, ref, self.p.sib).wait_recv()

    def forward1(self):
        p = self.p
        la, rb = self.half(p.at(-1), 0), self.half(p.at(1), 1)
        self.arrived(0, la)
        self.more(5, la, p.right)
        self.arrived(1, rb)
        self.more(6, rb, p.left)
        self.more(7, la, p.sib)
        self.more(8, rb, p.sib)

    def forward2(self):
        p = self.p
        lb, ra = self.half(p.at(-1), 1), self.half(p.at(1), 0)
        self.arrived(2, lb)
        self.more(9, lb, p.sib)
        self.arrived(3, ra)
        self.more(10, ra, p.sib)

    def wait_sib(self):
        self.arrived(4, rows_at(self.whole, self.p.sib * self.rows, self.rows))

    def forward3(self):
        p = self.p
        oa, ob = self.half(p.at(2), 0), self.half(p.at(2), 1)
        self.arrived(5, oa)
        self.more(11, oa, p.sib)
        self.arrived(6, ob)
        self.more(12, ob, p.sib)

    def finish_near(self):
        p = self.p
        for i, d, h in ((7, -1, 0), (8, 1, 1), (9, -1, 1), (10, 1, 0)):
            self.arrived(i, self.half(p.at(d, True), h))

    def finish_far(self):
        p = self.p
        for i, h in ((11, 0), (12, 1)):
            self.arrived(i, self.half(p.at(2, True), h))

    def drain(self):
        for c in self.sends:
            c.wait_send()


class Scatter:
    def __init__(self, place, rows, bufs, ssem, rsem, index):
        self.p, self.rows = place, rows
        self.sib_out, self.sib_in, self.ring, self.xin, self.lin, self.rin, self.own = bufs
        self.s = lambda i: ssem.at[index, i]
        self.r = lambda i: rsem.at[index, i]
        self.sends = []

    def go(self, i, src, dst, to):
        c = send(src, dst, self.s(i), self.r(i), enc=to)
        c.start()
        self.sends.append(c)

    def arrived(self, i, dst):
        send(dst, dst, self.s(i), self.r(i), enc=self.p.sib).wait_recv()

    def block(self, ref, d, which=None):
        if which is None:
            return ref.at[d * self.rows:(d + 1) * self.rows]
        h = self.rows // 2
        return ref.at[d * self.rows + which * h:d * self.rows + (which + 1) * h]

    def start(self, compute):
        p = self.p
        for d in (2, 1, 3, 0):
            self.block(self.sib_out, d)[...] = compute(p.at(d, True)).astype(BF)
            self.go(d, self.block(self.sib_out, d), self.block(self.sib_in, d), p.sib)
        for d in (2, 1, 3, 0):
            mine = compute(p.at(d))
            other = self.block(self.sib_in, d)
            self.arrived(d, other)
            mine = mine + other[...].astype(F32)
            if d == 0:
                self.own[...] = mine
                continue
            self.block(self.ring, d)[...] = mine.astype(BF)
            if d == 2:
                self.go(4, self.block(self.ring, 2, 0), self.block(self.xin, 0, 0), p.right)
                self.go(5, self.block(self.ring, 2, 1), self.block(self.xin, 0, 1), p.left)
            if d == 1:
                self.go(6, self.block(self.ring, 1, 1), self.block(self.lin, 0, 1), p.right)
            if d == 3:
                self.go(7, self.block(self.ring, 3, 0), self.block(self.rin, 0, 0), p.left)

    def mid(self):
        p = self.p
        for i, d, h, dst, to in ((4, 1, 0, self.lin, p.right), (5, 3, 1, self.rin, p.left)):
            came, mine = self.block(self.xin, 0, h), self.block(self.ring, d, h)
            self.arrived(i, came)
            mine[...] = (mine[...].astype(F32) + came[...].astype(F32)).astype(BF)
            self.go(i + 4, mine, self.block(dst, 0, h), to)

    def finish(self):
        self.arrived(6, self.block(self.lin, 0, 1))
        self.arrived(7, self.block(self.rin, 0, 0))
        self.arrived(8, self.block(self.lin, 0, 0))
        self.arrived(9, self.block(self.rin, 0, 1))

    def drain(self):
        for c in self.sends:
            c.wait_send()


class Ring:
    def __init__(self, block, half, bufs, plus, minus, ssem, rsem, index):
        self.block, self.half, self.plus, self.minus = block, half, plus, minus
        self.xin, self.lin, self.rin = bufs
        self.s = lambda i: ssem.at[index, i]
        self.r = lambda i: rsem.at[index, i]
        self.sends = []

    def go(self, i, src, dst, to):
        c = send(src, dst, self.s(i), self.r(i), dp=to)
        c.start()
        self.sends.append(c)

    def arrived(self, i, dst):
        send(dst, dst, self.s(i), self.r(i), dp=self.plus).wait_recv()

    def start(self):
        self.go(0, self.block(2, 0), self.half(self.xin, 0), self.plus)
        self.go(1, self.block(2, 1), self.half(self.xin, 1), self.minus)
        self.go(2, self.block(1, 1), self.half(self.lin, 1), self.plus)
        self.go(3, self.block(3, 0), self.half(self.rin, 0), self.minus)

    def mid(self):
        for i, d, h, dst, to in ((0, 1, 0, self.lin, self.plus), (1, 3, 1, self.rin, self.minus)):
            came, mine = self.half(self.xin, h), self.block(d, h)
            self.arrived(i, came)
            mine[...] = (mine[...].astype(F32) + came[...].astype(F32)).astype(BF)
            self.go(4 + i, mine, self.half(dst, h), to)

    def finish(self):
        self.arrived(2, self.half(self.lin, 1))
        self.arrived(3, self.half(self.rin, 0))
        self.arrived(4, self.half(self.lin, 0))
        self.arrived(5, self.half(self.rin, 1))

    def drain(self):
        for c in self.sends:
            c.wait_send()


class Plane:
    def __init__(self, out, bufs, ssem, rsem, index):
        n = lax.axis_size("dp")
        side = math.isqrt(n)
        me = lax.axis_index("dp")
        z, x = me // side, lax.rem(me, side)
        self.out, self.z, self.x = out, z, x
        rows, cols = out.shape[2], out.shape[3] // 2
        self.cols = cols

        def step_x(d):
            return lax.rem(x + d, side)

        def step_z(d):
            return lax.rem(z + d, side)

        along_x = (z * side + step_x(1), z * side + step_x(side - 1))
        along_z = (step_z(1) * side + x, step_z(side - 1) * side + x)
        two = lambda h: slice(2 * h, 2 * h + 2)
        part = lambda h: slice(h * rows // 2, (h + 1) * rows // 2)
        first, second, self.mids = bufs[0:6], bufs[6:12], bufs[12:14]
        half1 = lambda ref, h: ref.at[two(h)]
        half2 = lambda ref, h: ref.at[part(h)]
        self.first = [
            Ring(lambda d, h: out.at[two(h), step_x(d), :, :cols], half1, first[:3], *along_x,
                 ssem, rsem, index),
            Ring(lambda d, h: out.at[step_z(d), two(h), :, cols:], half1, first[3:], *along_z,
                 ssem, rsem, index + 1),
        ]
        self.second = [
            Ring(lambda d, h: self.mids[0].at[step_z(d), part(h)], half2, second[:3], *along_z,
                 ssem, rsem, index + 2),
            Ring(lambda d, h: self.mids[1].at[step_x(d), part(h)], half2, second[3:], *along_x,
                 ssem, rsem, index + 3),
        ]

    def start(self):
        for ring in self.first:
            ring.start()

    def mid(self):
        for ring in self.first:
            ring.mid()

    def turn(self):
        for i, ring in enumerate(self.first):
            ring.finish()
            own = (self.out[:, self.x, :, :self.cols] if i == 0
                   else self.out[self.z, :, :, self.cols:])
            self.mids[i][...] = (own.astype(F32) + ring.lin[...].astype(F32)
                                 + ring.rin[...].astype(F32)).astype(BF)
        for ring in self.second:
            ring.start()

    def mid2(self):
        for ring in self.second:
            ring.mid()

    def finish(self):
        got = []
        for i, ring in enumerate(self.second):
            ring.finish()
            own = self.mids[i][self.z if i == 0 else self.x]
            got.append(own.astype(F32) + ring.lin[...].astype(F32) + ring.rin[...].astype(F32))
        return got

    def drain(self):
        for ring in self.first + self.second:
            ring.drain()


def plane_bufs(side, rows, cols):
    return [((side, rows, cols), BF)] * 6 + [((rows, cols), BF)] * 6 + [((side, rows, cols), BF)] * 2


def scatter_bufs(rows, n):
    return [((4 * rows, n), BF)] * 3 + [((rows, n), BF)] * 3 + [((rows, n), F32)]


class Exchange:
    def __init__(self, src, dst, rows, ssem, rsem, index):
        self.src, self.dst, self.rows = src, dst, rows
        self.n = lax.axis_size("dp")
        self.me = lax.axis_index("dp")
        self.ssem, self.rsem, self.index = ssem, rsem, index

    def at(self, ref, i):
        return ref.at[i] if self.rows is None else rows_at(ref, i * self.rows, self.rows)

    def copy(self, j):
        to = lax.rem(self.me + j, self.n)
        return send(self.at(self.src, to), self.at(self.dst, self.me),
                    self.ssem.at[self.index, j], self.rsem.at[self.index, j], dp=to)

    def start(self):
        def body(j, carry):
            self.copy(j).start()
            return carry
        lax.fori_loop(1, self.n, body, 0)
        self.at(self.dst, self.me)[...] = self.at(self.src, self.me)[...]

    def wait(self):
        def body(j, carry):
            came = self.at(self.dst, lax.rem(self.me - j + self.n, self.n))
            send(came, came, self.ssem.at[self.index, j], self.rsem.at[self.index, j],
                 dp=lax.rem(self.me + 1, self.n)).wait_recv()
            return carry
        lax.fori_loop(1, self.n, body, 0)

    def drain(self):
        def body(j, carry):
            self.copy(j).wait_send()
            return carry
        lax.fori_loop(1, self.n, body, 0)


def chunks(count, step, body):
    def run(i, carry):
        body(pl.ds(pl.multiple_of(i * step, step), step), i * step)
        return carry
    lax.fori_loop(0, count // step, run, 0)


INPUTS = ("features", "weight_in", "bias", "proj", "pbias", "slot", "d_tokens", "requests")
OUTPUTS = ("tokens", "d_features", "d_high", "d_proj")


def step_kernel(names, *refs):
    r = dict(zip(INPUTS + OUTPUTS + names, refs))
    place = Place()
    n_dp, me = lax.axis_size("dp"), lax.axis_index("dp")
    filters, words = r["features"].shape
    total = r["whole0"].shape[0]
    c, tokens = r["d_tokens"].shape
    cap = r["requests"].shape[1]
    e = place.at(0)
    raw = pltpu.make_async_copy(r["weight_in"].at[0], r["raw"], r["raw_s"].at[0])
    raw.start()
    for o in range(n_dp):
        r["wanted"][o] = r["requests"][o:o + 1, :]

    barrier = pltpu.get_barrier_semaphore()
    for to in (place.left, place.right, place.sib):
        pl.semaphore_signal(barrier, inc=1, device_id={"enc": to}, device_id_type=MESH)

    def greet(j, carry):
        pl.semaphore_signal(barrier, inc=1, device_id={"dp": lax.rem(me + j, n_dp)},
                            device_id_type=MESH)
        return carry
    lax.fori_loop(1, n_dp, greet, 0)

    own_rows = pl.ds(pl.multiple_of(e * filters, filters), filters)
    r["whole0"][own_rows, :] = r["features"][...]
    pl.semaphore_wait(barrier, 3 + n_dp - 1)

    gather = [Gather(place, r["whole0"], filters, r["ag_s"], r["ag_r"], 0),
              Gather(place, r["whole1"], filters, r["ag_s"], r["ag_r"], 1),
              Gather(place, r["grads"], c, r["ag_s"], r["ag_r"], 2)]
    half = words // 2
    cols = [slice(0, half), slice(half, words)]
    sums = [[Scatter(place, filters, [r[f"rs{0 if j in (0, 2) else l}{h}_{j}"] for j in range(7)],
                     r["rs_s"], r["rs_r"], 2 * l + h) for h in range(2)] for l in range(2)]
    proj_sum = Scatter(place, c, [r[f"rs2_{j}"] for j in range(7)], r["rs_s"], r["rs_r"], 4)
    high_rows = total // n_dp
    proj_rows = r["proj"].shape[1] // n_dp

    def exchange(src, dst, rows, index):
        return Exchange(r[src], r[dst], rows, r["dp_s"], r["dp_r"], index)

    asked = exchange("wanted", "asked", None, 0)
    slots = exchange("slot_out", "slot_in", c, 1)
    picked = exchange("pick_out", "pick_in", c, 2)
    d_proj = exchange("dp_out", "dp_in", proj_rows, 3)
    d_high = [Plane(r[f"dh{l}_out"], [r[f"dh{l}_{j}"] for j in range(14)], r["ring_s"], r["ring_r"], 4 * l)
              for l in range(2)]

    gather[0].start()
    asked.start()

    def unpack(l):
        raw.wait()

        def body(at, start):
            r["weight"][l, at, :] = r["raw"][at].reshape(64, 2 * filters)
        chunks(total, 64, body)

    unpack(0)
    raw = pltpu.make_async_copy(r["weight_in"].at[1], r["raw"], r["raw_s"].at[1])
    raw.start()

    def layer(l, gat, whole, before, between, next_ref):
        acc, weight = r["acc"], r["weight"]

        def add(block, first=False):
            at = pl.ds(pl.multiple_of(block * filters, filters), filters)
            part = tn(weight[l, at, :], whole[at, :])
            acc[...] = part if first else acc[...] + part

        if l == 1:
            unpack(1)
        add(e, True)
        if before is not None:
            before()
        gat.forward1()
        between()
        gat.wait_sib()
        add(place.sib)
        gat.forward2()

        def near(i, carry):
            add(place.at(2 * i - 1))
            return carry
        lax.fori_loop(0, 2, near, 0)
        gat.forward3()
        if l == 1:
            gather[2].forward1()
        add(place.at(2))
        gat.finish_near()
        if l == 1:
            gather[2].forward2()

        def near_other(i, carry):
            add(place.at(2 * i - 1, True))
            return carry
        lax.fori_loop(0, 2, near_other, 0)
        gat.finish_far()
        if l == 1:
            gather[2].forward3()
        add(place.at(2, True))
        for i in range(2):
            r["bcol"][i * filters:(i + 1) * filters, :] = jnp.broadcast_to(
                r["bias"][l, i:i + 1, :], (128, filters)).T

        def mix(at, start):
            low = pl.ds(pl.multiple_of(filters + start, 32), 32)
            t = acc[at, :] + jnp.tile(r["bcol"][at, :], (1, words // 128))
            g = jax.nn.sigmoid(acc[low, :] + jnp.tile(r["bcol"][low, :], (1, words // 128)))
            r["t"][l, at, :] = t
            r["g"][l, at, :] = g
            h = whole[pl.ds(pl.multiple_of(e * filters + start, 32), 32), :].astype(F32)
            out = (g * (t * jax.nn.sigmoid(t)) + (1.0 - g) * h).astype(BF)
            if next_ref is r["top"]:
                next_ref[at, :] = out
            else:
                next_ref[pl.ds(pl.multiple_of(e * filters + start, 32), 32), :] = out
        chunks(filters, 32, mix)
        gat.drain()

    n_chunks = tokens // 1024
    r["sacc"][...] = jnp.zeros_like(r["sacc"])

    def slot_part(first, last):
        def body(i, carry):
            at = pl.ds(pl.multiple_of(i * 1024, 1024), 1024)
            slot = r["slot"][:, at]
            hot = one_hot(slot & 255, 256)
            high = slot >> 8
            d = r["d_tokens"][:, at]
            parts = [d * jnp.where(high == o, 1.0, 0.0).astype(BF) for o in range(n_dp)]
            r["sacc"][...] += nt(jnp.concatenate(parts, axis=0), hot)
            return carry
        lax.fori_loop(first, last, body, 0)

    def slot_rest():
        slot_part(n_chunks // 2, n_chunks)
        r["slot_out"][...] = r["sacc"][...].astype(BF)
        slots.start()

    layer(0, gather[0], r["whole0"], lambda: slot_part(0, n_chunks // 2), slot_rest, r["whole1"])
    gather[1].start()
    asked.wait()
    for o in range(n_dp):
        r["asked2"][o:o + 1, :] = r["asked"][o]

    def owner_part():
        slots.wait()
        owner_sums(r["asked2"], r["slot_in"], r["row"])
        r["grads"][pl.ds(pl.multiple_of(e * c, c), c), :] = r["row"][...]
        gather[2].start()

    layer(1, gather[1], r["whole1"], None, owner_part, r["top"])

    top, proj, up, acc = r["top"], r["proj"], r["up"], r["acc"]

    def own(start):
        return pl.ds(pl.multiple_of(e * filters + start, 32), 32)

    def cell(l, h):
        whole, at_h = r[f"whole{l}"], cols[h]

        def body(at, start):
            t, g, u = r["t"][l, at, at_h], r["g"][l, at, at_h], up[at, at_h]
            old = whole[own(start), at_h].astype(F32)
            s = jax.nn.sigmoid(t)
            r["pre"][l, at, at_h] = (u * g * (s * (1.0 + t * (1.0 - s)))).astype(BF)
            low = pl.ds(pl.multiple_of(filters + start, 32), 32)
            r["pre"][l, low, at_h] = (u * (t * s - old) * g * (1.0 - g)).astype(BF)
            up[at, at_h] = u * (1.0 - g)
        chunks(filters, 32, body)

    def back(l, h):
        return lambda dest: nn(
            r["weight"][l, pl.ds(pl.multiple_of(dest * filters, filters), filters), :],
            r["pre"][l, :, cols[h]])

    def add_up(l, h):
        s = sums[l][h]
        s.finish()

        def body(at, start):
            up[at, cols[h]] += s.own[at, :] + s.lin[at, :].astype(F32) + s.rin[at, :].astype(F32)
        chunks(filters, 32, body)

    def high_term(l):
        out = r[f"dh{l}_out"]
        side = out.shape[0]

        def body(z, carry):
            for x in range(0, side, 2):
                at = pl.ds(pl.multiple_of((z * side + x) * high_rows, 2 * high_rows), 2 * high_rows)
                got = nt(r[f"whole{l}"][at, :], r["pre"][l]).astype(BF)
                out[z, x:x + 2] = got.reshape(2, high_rows, 2 * filters)
            return carry
        lax.fori_loop(0, side, body, 0)
        d_high[l].start()

    def high_sum(l):
        for i, got in enumerate(d_high[l].finish()):
            r["d_high"][l, :, i, :] = got

    gather[2].wait_sib()
    gather[2].finish_near()
    gather[2].finish_far()
    for h in range(2):
        up[:, cols[h]] = nn(proj[...], r["grads"][:, cols[h]])
        cell(1, h)
        sums[1][h].start(back(1, h))
    acc[...] = tn(proj[...], top[...])
    sums[1][0].mid()
    proj_sum.start(lambda dest: acc[pl.ds(pl.multiple_of(dest * c, c), c), :])
    sums[1][1].mid()
    high_term(1)
    proj_sum.mid()
    add_up(1, 0)
    cell(0, 0)
    sums[1][0].drain()
    sums[0][0].start(back(0, 0))
    d_high[1].mid()
    add_up(1, 1)
    cell(0, 1)
    sums[1][1].drain()
    high_term(0)
    sums[0][0].mid()
    sums[0][1].start(back(0, 1))
    proj_sum.finish()
    r["encoded"][...] = (
        proj_sum.own[...] + proj_sum.lin[...].astype(F32) + proj_sum.rin[...].astype(F32)
        + column(jnp.concatenate([r["pbias"][...], jnp.zeros((1, 128 - c), F32)], axis=1))[:c]).astype(BF)
    owner_pick(r["asked2"], r["encoded"], r["pick_out"])
    picked.start()
    d_high[1].turn()
    sums[0][1].mid()
    d_high[0].mid()
    d_high[1].mid2()
    r["dp_out"][...] = nt(r["grads"][...], top[...]).astype(BF)
    d_proj.start()
    d_high[0].turn()
    high_sum(1)
    picked.wait()
    token_pick(r["slot"], r["pick_in"], r["tokens"])
    d_high[0].mid2()
    add_up(0, 0)
    add_up(0, 1)
    r["d_features"][...] = up[...].T.astype(BF)
    d_proj.wait()
    got = jnp.zeros((proj_rows, filters), F32)
    for i in range(n_dp):
        got = got + r["dp_in"][i * proj_rows:(i + 1) * proj_rows, :].astype(F32)
    r["d_proj"][...] = got
    high_sum(0)
    for x in (asked, slots, picked, d_proj, d_high[0], d_high[1], gather[2], *sums[0], proj_sum):
        x.drain()


def step(features, weight, bias, proj, pbias, slot, d_tokens, requests, n_dp):
    filters, words = features.shape
    total = weight.shape[1]
    c, tokens = d_tokens.shape
    width = proj.shape[1]
    cap = requests.shape[1]
    bufs = {
        "whole0": ((total, words), BF), "whole1": ((total, words), BF), "grads": ((width, words), BF),
        "top": ((filters, words), BF), "acc": ((2 * filters, words), F32),
        "bcol": ((2 * filters, 128), F32),
        "t": ((2, filters, words), F32), "g": ((2, filters, words), F32),
        "pre": ((2, 2 * filters, words), BF), "up": ((filters, words), F32),
        "sacc": ((n_dp * c, cap), F32),
        "slot_out": ((n_dp * c, cap), BF), "slot_in": ((n_dp * c, cap), BF),
        "pick_out": ((n_dp * c, cap), BF), "pick_in": ((n_dp * c, cap), BF),
        "row": ((c, words), BF), "encoded": ((c, words), BF),
        "dp_out": ((width, filters), BF), "dp_in": ((width, filters), BF),
        "weight": ((2, total, 2 * filters), BF), "raw": ((total, 2, filters), BF),
        "wanted": ((n_dp, 1, cap), jnp.int32), "asked": ((n_dp, 1, cap), jnp.int32), "asked2": ((n_dp, cap), jnp.int32),
    }
    for l in range(2):
        side = math.isqrt(n_dp)
        bufs[f"dh{l}_out"] = ((side, side, total // n_dp, 2 * filters), BF)
        for j, spec in enumerate(plane_bufs(side, total // n_dp, filters)):
            bufs[f"dh{l}_{j}"] = spec
    for l in range(2):
        for h in range(2):
            for j, spec in enumerate(scatter_bufs(filters, words // 2)):
                if l != 1 or j not in (0, 2):
                    bufs[f"rs{l}{h}_{j}"] = spec
    for j, spec in enumerate(scatter_bufs(c, words)):
        bufs[f"rs2_{j}"] = spec
    scratch = [pltpu.VMEM(*spec) for spec in bufs.values()]
    sems = {"ag": (3, 13), "rs": (5, 10), "dp": (4, n_dp), "ring": (8, 6), "raw": (2,)}
    names = tuple(bufs)
    for name, dims in sems.items():
        names += (name + "_s", name + "_r")
        scratch += [pltpu.SemaphoreType.DMA(dims)] * 2
    return pl.pallas_call(
        functools.partial(step_kernel, names),
        in_specs=[pl.BlockSpec(memory_space=pl.ANY) if x == "weight_in" else VM for x in INPUTS], out_specs=[VM] * len(OUTPUTS),
        out_shape=[
            jax.ShapeDtypeStruct((c, tokens), BF),
            jax.ShapeDtypeStruct((words, filters), BF),
            jax.ShapeDtypeStruct((2, total // n_dp, 2, filters), F32),
            jax.ShapeDtypeStruct((width // n_dp, filters), F32),
        ],
        scratch_shapes=scratch,
        compiler_params=pltpu.CompilerParams(
            collective_id=0, has_side_effects=True, vmem_limit_bytes=62 << 20),
    )(features, weight, bias, proj, pbias, slot, d_tokens, requests)


def hand_on(*arrays):
    n = len(arrays)

    def kernel(*refs):
        for i in range(n):
            refs[n + i][...] = refs[i][...]

    return pl.pallas_call(
        kernel, in_specs=[VM] * n, out_specs=[VM] * n,
        out_shape=[jax.ShapeDtypeStruct(a.shape, a.dtype) for a in arrays],
        compiler_params=pltpu.CompilerParams(vmem_limit_bytes=63 << 20),
    )(*arrays)


def per_device(chars, char_table, conv_weight, conv_bias, hw_weight, hw_bias, proj_weight,
               proj_bias, owner_types, requests, tok_slot, d_tokens):
    taps, embed_width, filters = conv_weight.shape
    layers, total = hw_weight.shape[:2]
    unique = owner_types.shape[0]
    owners, cap = requests.shape[1:]
    tokens, c = d_tokens.shape
    features = encode(chars.T, owner_types.reshape(1, unique), char_table.T,
                      conv_weight.reshape(taps * embed_width, filters),
                      conv_bias.reshape(1, filters), total)
    outs = step(
        features, hw_weight, hw_bias, proj_weight, proj_bias.reshape(1, c),
        tok_slot.reshape(1, tokens), d_tokens.T, requests.reshape(owners, cap), owners)
    tok, d_feat, d_high, d_proj = hand_on(*outs)
    return tok.T, d_feat, d_high, d_proj.T


def solution(mesh):
    return jax.shard_map(
        per_device,
        mesh=mesh,
        in_specs=(
            P("dp", None), P(), P(None, None, "enc"), P("enc"), P(None, None, None, "enc"),
            P(None, None, "enc"), P("enc", None), P("enc"), P("dp"), P("dp", None, None),
            P("dp"), P("dp", "enc"),
        ),
        out_specs=(P("dp", "enc"), P("dp", "enc"), P(None, "dp", None, "enc"), P("enc", "dp")),
        check_vma=False,
    )
```

```python
import math
import functools
import jax
import jax.numpy as jnp
from jax import lax
from jax.experimental import pallas as pl
from jax.experimental.pallas import tpu as pltpu
from jax.sharding import PartitionSpec as P

BF = jnp.bfloat16
F32 = jnp.float32
VM = pl.BlockSpec(memory_space=pltpu.VMEM)
BASE = 128


def width_of(index, total):
    width = jnp.ones(index.shape, jnp.int32)
    for share in (1, 2, 4, 8, 16, 32):
        width = width + (index >= share * total // 64).astype(jnp.int32)
    return width


def one_hot(row, count):
    n = row.shape[1]
    return jnp.where(
        lax.broadcasted_iota(jnp.int32, (count, n), 0) == row, 1.0, 0.0
    ).astype(BF)


def nt(a, b):
    return lax.dot_general(a, b, (((1,), (1,)), ((), ())), preferred_element_type=F32)


def nn(a, b):
    return jnp.dot(a, b, preferred_element_type=F32)


def tn(a, b):
    return lax.dot_general(a, b, (((0,), (0,)), ((), ())), preferred_element_type=F32)


def column(row):
    return jnp.broadcast_to(row, (128, row.shape[1])).T[:, :1]


def encode_kernel(total, length, chars_ref, types_ref, letters_ref, weight_ref, bias_ref,
                  out_ref, hot, lhs, acc, vec, band, best, table_ref):
    step = pl.program_id(0)
    words = types_ref.shape[1]
    lanes = 256
    group = chars_ref.shape[1] // lanes
    rows = 64

    @pl.when(step == 0)
    def _():
        hot[...] = one_hot(types_ref[...] & (lanes - 1), lanes)
        acc[...] = jnp.zeros_like(acc)
        lhs[...] = jnp.zeros_like(lhs)
        table_ref[...] = jnp.zeros_like(table_ref)
        table_ref[:, :letters_ref.shape[1]] = letters_ref[...].astype(F32)

    high = types_ref[...] // lanes
    for part in range(group // 8):
        for j in range(8):
            block = chars_ref[:, (part * 8 + j) * lanes:(part * 8 + j + 1) * lanes]
            lhs[j * rows:j * rows + length, :] = (block - BASE).astype(F32).astype(BF)
        for half in range(words // 256):
            cols = slice(half * 256, half * 256 + 256)
            picked = nn(lhs[...], hot[:, cols])
            here = acc[:, cols]
            for j in range(8):
                here = jnp.where(high[:, cols] == step * group + part * 8 + j,
                                 picked[j * rows:(j + 1) * rows], here)
            acc[:, cols] = here

    @pl.when(step == pl.num_programs(0) - 1)
    def _():
        filters = weight_ref.shape[1]
        vec[length * 16:, :] = jnp.zeros((vec.shape[0] - length * 16, words), BF)

        def embed(p, carry):
            row = acc[pl.ds(p, 1), :].astype(jnp.int32) + BASE
            for b in range(words // 128):
                idx = jnp.broadcast_to(row[:, b * 128:(b + 1) * 128], (8, 128))
                low, seg = idx & 127, idx >> 7
                halves = []
                for h in range(2):
                    got = None
                    for s in range(3):
                        tab = table_ref[h * 8:(h + 1) * 8, s * 128:(s + 1) * 128]
                        val = jnp.take_along_axis(tab, low, axis=1)
                        got = val if got is None else jnp.where(seg == s, val, got)
                    halves.append(got)
                vec[pl.ds(pl.multiple_of(p * 16, 16), 16), b * 128:(b + 1) * 128] = (
                    jnp.concatenate(halves, axis=0).astype(BF))
            return carry

        lax.fori_loop(0, length, embed, 0, unroll=10)

        base = lax.axis_index("enc") * filters
        width_row = width_of(base + lax.broadcasted_iota(jnp.int32, (128, filters), 1), total)
        tap = lax.broadcasted_iota(jnp.int32, (128, filters), 0) // 16
        raw = jnp.concatenate(
            [weight_ref[...].astype(F32), jnp.zeros((128 - weight_ref.shape[0], filters), F32)],
            axis=0)
        kt = jnp.where(tap < width_row, raw, 0.0).T
        wide = jnp.concatenate([kt, jnp.zeros((filters, 128), F32)], axis=1)
        for q in range(8):
            moved = wide if q == 0 else pltpu.roll(wide, q * 16, 1)
            band[q * filters:(q + 1) * filters, :] = moved.astype(BF)
        best[...] = jnp.full(best.shape, -jnp.inf, F32)
        width_col = width_of(base + lax.broadcasted_iota(jnp.int32, (filters, 256), 0), total)
        groups = -(-length // 8)

        def conv(g, first, count, masked):
            for half in range(words // 256):
                cols = slice(half * 256, half * 256 + 256)
                win = vec[pl.ds(pl.multiple_of(g * 128, 128), 256), cols]
                out = nn(band[:count * filters, :], win)
                m = best[:, cols]
                for q in range(count):
                    val = out[q * filters:(q + 1) * filters]
                    if masked and first + q + 7 > length:
                        val = jnp.where(width_col <= length - first - q, val, -jnp.inf)
                    m = jnp.maximum(m, val)
                best[:, cols] = m

        def body(g, carry):
            conv(g, 0, 8, False)
            return carry

        lax.fori_loop(0, groups - 2, body, 0)
        for g in (groups - 2, groups - 1):
            conv(g, g * 8, min(8, length - g * 8), True)
        out_ref[...] = jnp.maximum(best[...] + column(bias_ref[...]), 0.0).astype(BF)


def encode(chars_t, types, table_t, weight, bias, total):
    length, count = chars_t.shape
    words = types.shape[1]
    filters = weight.shape[1]
    block = 8192
    return pl.pallas_call(
        functools.partial(encode_kernel, total, length),
        grid=(count // block,),
        in_specs=[pl.BlockSpec((length, block), lambda i: (0, i)), VM, VM, VM, VM],
        out_specs=VM,
        out_shape=jax.ShapeDtypeStruct((filters, words), BF),
        scratch_shapes=[
            pltpu.VMEM((256, words), BF),
            pltpu.VMEM((512, 256), BF),
            pltpu.VMEM((64, words), F32),
            pltpu.VMEM((1024, words), BF),
            pltpu.VMEM((8 * filters, 256), BF),
            pltpu.VMEM((filters, words), F32),
            pltpu.VMEM((16, 384), F32),
        ],
        compiler_params=pltpu.CompilerParams(vmem_limit_bytes=63 << 20),
    )(chars_t, types, table_t, weight, bias)


def slot_sums(slot_ref, d_ref, out_ref, acc, chunk=1024):
    c, tokens = d_ref.shape
    owners = out_ref.shape[0] // c
    acc[...] = jnp.zeros_like(acc)

    def body(i, carry):
        at = pl.ds(pl.multiple_of(i * chunk, chunk), chunk)
        slot = slot_ref[:, at]
        hot = one_hot(slot & 255, 256)
        high = slot >> 8
        d = d_ref[:, at]
        parts = [d * jnp.where(high == o, 1.0, 0.0).astype(BF) for o in range(owners)]
        acc[...] += nt(jnp.concatenate(parts, axis=0), hot)
        return carry

    lax.fori_loop(0, tokens // chunk, body, 0)
    out_ref[...] = acc[...].astype(BF)


def token_pick(slot_ref, ret_ref, out_ref, chunk=1024):
    c, tokens = out_ref.shape
    owners = ret_ref.shape[0] // c

    def body(i, carry):
        at = pl.ds(pl.multiple_of(i * chunk, chunk), chunk)
        slot = slot_ref[:, at]
        got = nn(ret_ref[...], one_hot(slot & 255, 256))
        high = slot >> 8
        out = jnp.zeros((c, chunk), F32)
        for o in range(owners):
            out = jnp.where(high == o, got[o * c:(o + 1) * c], out)
        out_ref[:, at] = out.astype(BF)
        return carry

    lax.fori_loop(0, tokens // chunk, body, 0)


def owner_sums(asked_ref, arr_ref, out_ref):
    c, unique = out_ref.shape
    reps, cap = asked_ref.shape
    acc = jnp.zeros((unique // 256 * c, 256), F32)
    for r in range(reps):
        asked = asked_ref[r:r + 1, :]
        hot = one_hot(asked & 255, 256)
        a = arr_ref[r * c:(r + 1) * c, :]
        parts = [a * jnp.where((asked >> 8) == h, 1.0, 0.0).astype(BF) for h in range(unique // 256)]
        acc += nt(jnp.concatenate(parts, axis=0), hot)
    for h in range(unique // 256):
        out_ref[:, h * 256:(h + 1) * 256] = acc[h * c:(h + 1) * c].astype(BF)


def owner_pick(asked_ref, enc_ref, out_ref):
    c, unique = enc_ref.shape
    reps, cap = asked_ref.shape
    enc = enc_ref[...]
    tall = jnp.concatenate([enc[:, h * 256:(h + 1) * 256] for h in range(unique // 256)], axis=0)
    for r in range(reps):
        asked = asked_ref[r:r + 1, :]
        got = nn(tall, one_hot(asked & 255, 256))
        out = jnp.zeros((c, cap), F32)
        for h in range(unique // 256):
            out = jnp.where((asked >> 8) == h, got[h * c:(h + 1) * c], out)
        out_ref[r * c:(r + 1) * c, :] = out.astype(BF)


def local(body, shape, scratch, *args):
    return pl.pallas_call(
        body, in_specs=[VM] * len(args), out_specs=VM,
        out_shape=jax.ShapeDtypeStruct(shape, BF), scratch_shapes=scratch,
        compiler_params=pltpu.CompilerParams(vmem_limit_bytes=48 << 20),
    )(*args)


MESH = pl.DeviceIdType.MESH


def send(src, dst, ssem, rsem, **to):
    return pltpu.make_async_remote_copy(
        src_ref=src, dst_ref=dst, send_sem=ssem, recv_sem=rsem, device_id=to, device_id_type=MESH)


def rows_at(ref, start, count):
    return ref.at[pl.ds(pl.multiple_of(start, count), count)]


class Place:
    def __init__(self):
        e = lax.axis_index("enc")
        self.chips = lax.axis_size("enc") // 2
        self.y, self.k = e // 2, lax.rem(e, 2)
        self.sib = self.y * 2 + 1 - self.k
        self.right = self.at(1)
        self.left = self.at(-1)

    def at(self, d, other=False):
        yy = lax.rem(self.y + d + self.chips, self.chips)
        return yy * 2 + (1 - self.k if other else self.k)


class Gather:
    def __init__(self, place, whole, rows, ssem, rsem, index):
        self.p, self.whole, self.rows = place, whole, rows
        self.s = lambda i: ssem.at[index, i]
        self.r = lambda i: rsem.at[index, i]

    def half(self, e, which):
        h = self.rows // 2
        return rows_at(self.whole, e * self.rows + which * h, h)

    def copy(self, i, ref, to):
        return send(ref, ref, self.s(i), self.r(i), enc=to)

    def start(self):
        p = self.p
        own = p.at(0)
        self.sends = [
            self.copy(0, self.half(own, 0), p.right),
            self.copy(1, self.half(own, 1), p.left),
            self.copy(2, self.half(own, 1), p.right),
            self.copy(3, self.half(own, 0), p.left),
            self.copy(4, rows_at(self.whole, own * self.rows, self.rows), p.sib),
        ]
        for c in self.sends:
            c.start()

    def more(self, i, ref, to):
        c = self.copy(i, ref, to)
        c.start()
        self.sends.append(c)

    def arrived(self, i, ref):
        self.copy(i, ref, self.p.sib).wait_recv()

    def forward1(self):
        p = self.p
        la, rb = self.half(p.at(-1), 0), self.half(p.at(1), 1)
        self.arrived(0, la)
        self.more(5, la, p.right)
        self.arrived(1, rb)
        self.more(6, rb, p.left)
        self.more(7, la, p.sib)
        self.more(8, rb, p.sib)

    def forward2(self):
        p = self.p
        lb, ra = self.half(p.at(-1), 1), self.half(p.at(1), 0)
        self.arrived(2, lb)
        self.more(9, lb, p.sib)
        self.arrived(3, ra)
        self.more(10, ra, p.sib)

    def wait_sib(self):
        self.arrived(4, rows_at(self.whole, self.p.sib * self.rows, self.rows))

    def forward3(self):
        p = self.p
        oa, ob = self.half(p.at(2), 0), self.half(p.at(2), 1)
        self.arrived(5, oa)
        self.more(11, oa, p.sib)
        self.arrived(6, ob)
        self.more(12, ob, p.sib)

    def finish_near(self):
        p = self.p
        for i, d, h in ((7, -1, 0), (8, 1, 1), (9, -1, 1), (10, 1, 0)):
            self.arrived(i, self.half(p.at(d, True), h))

    def finish_far(self):
        p = self.p
        for i, h in ((11, 0), (12, 1)):
            self.arrived(i, self.half(p.at(2, True), h))

    def drain(self):
        for c in self.sends:
            c.wait_send()


class Scatter:
    def __init__(self, place, rows, bufs, ssem, rsem, index):
        self.p, self.rows = place, rows
        self.sib_out, self.sib_in, self.ring, self.xin, self.lin, self.rin, self.own = bufs
        self.s = lambda i: ssem.at[index, i]
        self.r = lambda i: rsem.at[index, i]
        self.sends = []

    def go(self, i, src, dst, to):
        c = send(src, dst, self.s(i), self.r(i), enc=to)
        c.start()
        self.sends.append(c)

    def arrived(self, i, dst):
        send(dst, dst, self.s(i), self.r(i), enc=self.p.sib).wait_recv()

    def block(self, ref, d, which=None):
        if which is None:
            return ref.at[d * self.rows:(d + 1) * self.rows]
        h = self.rows // 2
        return ref.at[d * self.rows + which * h:d * self.rows + (which + 1) * h]

    def start(self, compute):
        p = self.p
        for d in (2, 1, 3, 0):
            self.block(self.sib_out, d)[...] = compute(p.at(d, True)).astype(BF)
            self.go(d, self.block(self.sib_out, d), self.block(self.sib_in, d), p.sib)
        for d in (2, 1, 3, 0):
            mine = compute(p.at(d))
            other = self.block(self.sib_in, d)
            self.arrived(d, other)
            mine = mine + other[...].astype(F32)
            if d == 0:
                self.own[...] = mine
                continue
            self.block(self.ring, d)[...] = mine.astype(BF)
            if d == 2:
                self.go(4, self.block(self.ring, 2, 0), self.block(self.xin, 0, 0), p.right)
                self.go(5, self.block(self.ring, 2, 1), self.block(self.xin, 0, 1), p.left)
            if d == 1:
                self.go(6, self.block(self.ring, 1, 1), self.block(self.lin, 0, 1), p.right)
            if d == 3:
                self.go(7, self.block(self.ring, 3, 0), self.block(self.rin, 0, 0), p.left)

    def mid(self):
        p = self.p
        for i, d, h, dst, to in ((4, 1, 0, self.lin, p.right), (5, 3, 1, self.rin, p.left)):
            came, mine = self.block(self.xin, 0, h), self.block(self.ring, d, h)
            self.arrived(i, came)
            mine[...] = (mine[...].astype(F32) + came[...].astype(F32)).astype(BF)
            self.go(i + 4, mine, self.block(dst, 0, h), to)

    def finish(self):
        self.arrived(6, self.block(self.lin, 0, 1))
        self.arrived(7, self.block(self.rin, 0, 0))
        self.arrived(8, self.block(self.lin, 0, 0))
        self.arrived(9, self.block(self.rin, 0, 1))

    def drain(self):
        for c in self.sends:
            c.wait_send()


class Ring:
    def __init__(self, block, half, bufs, plus, minus, ssem, rsem, index):
        self.block, self.half, self.plus, self.minus = block, half, plus, minus
        self.xin, self.lin, self.rin = bufs
        self.s = lambda i: ssem.at[index, i]
        self.r = lambda i: rsem.at[index, i]
        self.sends = []

    def go(self, i, src, dst, to):
        c = send(src, dst, self.s(i), self.r(i), dp=to)
        c.start()
        self.sends.append(c)

    def arrived(self, i, dst):
        send(dst, dst, self.s(i), self.r(i), dp=self.plus).wait_recv()

    def start(self):
        self.go(0, self.block(2, 0), self.half(self.xin, 0), self.plus)
        self.go(1, self.block(2, 1), self.half(self.xin, 1), self.minus)
        self.go(2, self.block(1, 1), self.half(self.lin, 1), self.plus)
        self.go(3, self.block(3, 0), self.half(self.rin, 0), self.minus)

    def mid(self):
        for i, d, h, dst, to in ((0, 1, 0, self.lin, self.plus), (1, 3, 1, self.rin, self.minus)):
            came, mine = self.half(self.xin, h), self.block(d, h)
            self.arrived(i, came)
            mine[...] = (mine[...].astype(F32) + came[...].astype(F32)).astype(BF)
            self.go(4 + i, mine, self.half(dst, h), to)

    def finish(self):
        self.arrived(2, self.half(self.lin, 1))
        self.arrived(3, self.half(self.rin, 0))
        self.arrived(4, self.half(self.lin, 0))
        self.arrived(5, self.half(self.rin, 1))

    def drain(self):
        for c in self.sends:
            c.wait_send()


class Plane:
    def __init__(self, out, bufs, ssem, rsem, index):
        n = lax.axis_size("dp")
        side = math.isqrt(n)
        me = lax.axis_index("dp")
        z, x = me // side, lax.rem(me, side)
        self.out, self.z, self.x = out, z, x
        rows, cols = out.shape[2], out.shape[3] // 2
        self.cols = cols

        def step_x(d):
            return lax.rem(x + d, side)

        def step_z(d):
            return lax.rem(z + d, side)

        along_x = (z * side + step_x(1), z * side + step_x(side - 1))
        along_z = (step_z(1) * side + x, step_z(side - 1) * side + x)
        two = lambda h: slice(2 * h, 2 * h + 2)
        part = lambda h: slice(h * rows // 2, (h + 1) * rows // 2)
        first, second, self.mids = bufs[0:6], bufs[6:12], bufs[12:14]
        half1 = lambda ref, h: ref.at[two(h)]
        half2 = lambda ref, h: ref.at[part(h)]
        self.first = [
            Ring(lambda d, h: out.at[two(h), step_x(d), :, :cols], half1, first[:3], *along_x,
                 ssem, rsem, index),
            Ring(lambda d, h: out.at[step_z(d), two(h), :, cols:], half1, first[3:], *along_z,
                 ssem, rsem, index + 1),
        ]
        self.second = [
            Ring(lambda d, h: self.mids[0].at[step_z(d), part(h)], half2, second[:3], *along_z,
                 ssem, rsem, index + 2),
            Ring(lambda d, h: self.mids[1].at[step_x(d), part(h)], half2, second[3:], *along_x,
                 ssem, rsem, index + 3),
        ]

    def start(self):
        for ring in self.first:
            ring.start()

    def mid(self):
        for ring in self.first:
            ring.mid()

    def turn(self):
        for i, ring in enumerate(self.first):
            ring.finish()
            own = (self.out[:, self.x, :, :self.cols] if i == 0
                   else self.out[self.z, :, :, self.cols:])
            self.mids[i][...] = (own.astype(F32) + ring.lin[...].astype(F32)
                                 + ring.rin[...].astype(F32)).astype(BF)
        for ring in self.second:
            ring.start()

    def mid2(self):
        for ring in self.second:
            ring.mid()

    def finish(self):
        got = []
        for i, ring in enumerate(self.second):
            ring.finish()
            own = self.mids[i][self.z if i == 0 else self.x]
            got.append(own.astype(F32) + ring.lin[...].astype(F32) + ring.rin[...].astype(F32))
        return got

    def drain(self):
        for ring in self.first + self.second:
            ring.drain()


def plane_bufs(side, rows, cols):
    return [((side, rows, cols), BF)] * 6 + [((rows, cols), BF)] * 6 + [((side, rows, cols), BF)] * 2


def scatter_bufs(rows, n):
    return [((4 * rows, n), BF)] * 3 + [((rows, n), BF)] * 3 + [((rows, n), F32)]


WAVES = (
    ((0, 1), (0, 3), (1, 0), (3, 0)),
    ((1, 1), (3, 3), (1, 3), (3, 1)),
    ((0, 2), (2, 0), (2, 2)),
    ((1, 2), (2, 1), (3, 2), (2, 3)),
)


class Exchange:
    def __init__(self, src, dst, rows, ssem, rsem, index):
        self.src, self.dst, self.rows = src, dst, rows
        self.n = lax.axis_size("dp")
        self.me = lax.axis_index("dp")
        self.ssem, self.rsem, self.index = ssem, rsem, index

    def at(self, ref, i):
        return ref.at[i] if self.rows is None else rows_at(ref, i * self.rows, self.rows)

    def peer(self, step):
        side = math.isqrt(self.n)
        z, x = self.me // side, lax.rem(self.me, side)
        return (lax.rem(z + step[0] + side, side) * side + lax.rem(x + step[1] + side, side))

    def sems(self, step):
        at = step[0] * math.isqrt(self.n) + step[1]
        return self.ssem.at[self.index, at], self.rsem.at[self.index, at]

    def copy(self, step):
        to = self.peer(step)
        return send(self.at(self.src, to), self.at(self.dst, self.me), *self.sems(step), dp=to)

    def start(self):
        self.at(self.dst, self.me)[...] = self.at(self.src, self.me)[...]
        for group in WAVES:
            for step in group:
                self.copy(step).start()

    def wait(self):
        for group in WAVES:
            for step in group:
                came = self.at(self.dst, self.peer((-step[0], -step[1])))
                send(came, came, *self.sems(step), dp=self.peer((0, 1))).wait_recv()

    def drain(self):
        for group in WAVES:
            for step in group:
                self.copy(step).wait_send()


def chunks(count, step, body):
    def run(i, carry):
        body(pl.ds(pl.multiple_of(i * step, step), step), i * step)
        return carry
    lax.fori_loop(0, count // step, run, 0)


INPUTS = ("features", "weight_in", "bias", "proj", "pbias", "slot", "d_tokens", "requests")
OUTPUTS = ("tokens", "d_features", "d_high", "d_proj")


def step_kernel(names, *refs):
    r = dict(zip(INPUTS + OUTPUTS + names, refs))
    place = Place()
    n_dp, me = lax.axis_size("dp"), lax.axis_index("dp")
    filters, words = r["features"].shape
    total = r["whole0"].shape[0]
    c, tokens = r["d_tokens"].shape
    cap = r["requests"].shape[1]
    e = place.at(0)
    fetch = pltpu.make_async_copy(r["d_tokens"], r["dt"], r["raw_s"].at[2])
    fetch.start()
    raw = pltpu.make_async_copy(r["weight_in"].at[0], r["raw"], r["raw_s"].at[0])
    raw.start()
    for o in range(n_dp):
        r["wanted"][o] = r["requests"][o:o + 1, :]

    barrier = pltpu.get_barrier_semaphore()
    for to in (place.left, place.right, place.sib):
        pl.semaphore_signal(barrier, inc=1, device_id={"enc": to}, device_id_type=MESH)

    def greet(j, carry):
        pl.semaphore_signal(barrier, inc=1, device_id={"dp": lax.rem(me + j, n_dp)},
                            device_id_type=MESH)
        return carry
    lax.fori_loop(1, n_dp, greet, 0)

    own_rows = pl.ds(pl.multiple_of(e * filters, filters), filters)
    r["whole0"][own_rows, :] = r["features"][...]
    pl.semaphore_wait(barrier, 3 + n_dp - 1)

    gather = [Gather(place, r["whole0"], filters, r["ag_s"], r["ag_r"], 0),
              Gather(place, r["whole1"], filters, r["ag_s"], r["ag_r"], 1),
              Gather(place, r["grads"], c, r["ag_s"], r["ag_r"], 2)]
    half = words // 2
    cols = [slice(0, half), slice(half, words)]
    sums = [[Scatter(place, filters, [r[f"rs{0 if j in (0, 2) else l}{h}_{j}"] for j in range(7)],
                     r["rs_s"], r["rs_r"], 2 * l + h) for h in range(2)] for l in range(2)]
    proj_sum = Scatter(place, c, [r[f"rs2_{j}"] for j in range(7)], r["rs_s"], r["rs_r"], 4)
    high_rows = total // n_dp
    proj_rows = r["proj"].shape[1] // n_dp

    def exchange(src, dst, rows, index):
        return Exchange(r[src], r[dst], rows, r["dp_s"], r["dp_r"], index)

    asked = exchange("wanted", "asked", None, 0)
    slots = exchange("slot_out", "slot_in", c, 1)
    picked = exchange("pick_out", "pick_in", c, 2)
    d_proj = exchange("dp_out", "dp_in", proj_rows, 3)
    d_high = [Plane(r[f"dh{l}_out"], [r[f"dh{l}_{j}"] for j in range(14)], r["ring_s"], r["ring_r"], 4 * l)
              for l in range(2)]

    gather[0].start()
    asked.start()

    def unpack(l):
        raw.wait()

        def body(at, start):
            r["weight"][l, at, :] = r["raw"][at].reshape(64, 2 * filters)
        chunks(total, 64, body)

    unpack(0)
    raw = pltpu.make_async_copy(r["weight_in"].at[1], r["raw"], r["raw_s"].at[1])
    raw.start()

    def layer(l, gat, whole, before, between, next_ref):
        acc, weight = r["acc"], r["weight"]

        def add(block, first=False):
            at = pl.ds(pl.multiple_of(block * filters, filters), filters)
            part = tn(weight[l, at, :], whole[at, :])
            acc[...] = part if first else acc[...] + part

        if l == 1:
            unpack(1)
        add(e, True)
        if before is not None:
            before()
        gat.forward1()
        between()
        gat.wait_sib()
        add(place.sib)
        gat.forward2()

        def near(i, carry):
            add(place.at(2 * i - 1))
            return carry
        lax.fori_loop(0, 2, near, 0)
        gat.forward3()
        if l == 1:
            gather[2].forward1()
        add(place.at(2))
        gat.finish_near()
        if l == 1:
            gather[2].forward2()

        def near_other(i, carry):
            add(place.at(2 * i - 1, True))
            return carry
        lax.fori_loop(0, 2, near_other, 0)
        gat.finish_far()
        if l == 1:
            gather[2].forward3()
        add(place.at(2, True))
        for i in range(2):
            r["bcol"][i * filters:(i + 1) * filters, :] = jnp.broadcast_to(
                r["bias"][l, i:i + 1, :], (128, filters)).T

        def mix(at, start):
            low = pl.ds(pl.multiple_of(filters + start, 32), 32)
            t = acc[at, :] + jnp.tile(r["bcol"][at, :], (1, words // 128))
            g = jax.nn.sigmoid(acc[low, :] + jnp.tile(r["bcol"][low, :], (1, words // 128)))
            r["t"][l, at, :] = t
            r["g"][l, at, :] = g
            h = whole[pl.ds(pl.multiple_of(e * filters + start, 32), 32), :].astype(F32)
            out = (g * (t * jax.nn.sigmoid(t)) + (1.0 - g) * h).astype(BF)
            if next_ref is r["top"]:
                next_ref[at, :] = out
            else:
                next_ref[pl.ds(pl.multiple_of(e * filters + start, 32), 32), :] = out
        chunks(filters, 32, mix)
        gat.drain()

    n_chunks = tokens // 1024
    fetch.wait()
    r["sacc"][...] = jnp.zeros_like(r["sacc"])

    def slot_part(first, last):
        def body(i, carry):
            at = pl.ds(pl.multiple_of(i * 1024, 1024), 1024)
            slot = r["slot"][:, at]
            hot = one_hot(slot & 255, 256)
            high = slot >> 8
            d = r["dt"][:, at]
            parts = [d * jnp.where(high == o, 1.0, 0.0).astype(BF) for o in range(n_dp)]
            r["sacc"][...] += nt(jnp.concatenate(parts, axis=0), hot)
            return carry
        lax.fori_loop(first, last, body, 0)

    def slot_rest():
        slot_part(n_chunks // 2, n_chunks)
        r["slot_out"][...] = r["sacc"][...].astype(BF)
        slots.start()

    layer(0, gather[0], r["whole0"], lambda: slot_part(0, n_chunks // 2), slot_rest, r["whole1"])
    gather[1].start()
    asked.wait()
    for o in range(n_dp):
        r["asked2"][o:o + 1, :] = r["asked"][o]

    def owner_part():
        slots.wait()
        owner_sums(r["asked2"], r["slot_in"], r["row"])
        r["grads"][pl.ds(pl.multiple_of(e * c, c), c), :] = r["row"][...]
        gather[2].start()

    layer(1, gather[1], r["whole1"], None, owner_part, r["top"])

    top, proj, up, acc = r["top"], r["proj"], r["up"], r["acc"]

    def own(start):
        return pl.ds(pl.multiple_of(e * filters + start, 32), 32)

    def cell(l, h):
        whole, at_h = r[f"whole{l}"], cols[h]

        def body(at, start):
            t, g, u = r["t"][l, at, at_h], r["g"][l, at, at_h], up[at, at_h]
            old = whole[own(start), at_h].astype(F32)
            s = jax.nn.sigmoid(t)
            r["pre"][l, at, at_h] = (u * g * (s * (1.0 + t * (1.0 - s)))).astype(BF)
            low = pl.ds(pl.multiple_of(filters + start, 32), 32)
            r["pre"][l, low, at_h] = (u * (t * s - old) * g * (1.0 - g)).astype(BF)
            up[at, at_h] = u * (1.0 - g)
        chunks(filters, 32, body)

    def back(l, h):
        return lambda dest: nn(
            r["weight"][l, pl.ds(pl.multiple_of(dest * filters, filters), filters), :],
            r["pre"][l, :, cols[h]])

    def add_up(l, h):
        s = sums[l][h]
        s.finish()

        def body(at, start):
            up[at, cols[h]] += s.own[at, :] + s.lin[at, :].astype(F32) + s.rin[at, :].astype(F32)
        chunks(filters, 32, body)

    def high_term(l):
        out = r[f"dh{l}_out"]
        side = out.shape[0]

        def body(z, carry):
            for x in range(0, side, 2):
                at = pl.ds(pl.multiple_of((z * side + x) * high_rows, 2 * high_rows), 2 * high_rows)
                got = nt(r[f"whole{l}"][at, :], r["pre"][l]).astype(BF)
                out[z, x:x + 2] = got.reshape(2, high_rows, 2 * filters)
            return carry
        lax.fori_loop(0, side, body, 0)
        d_high[l].start()

    def high_sum(l):
        for i, got in enumerate(d_high[l].finish()):
            r["d_high"][l, :, i, :] = got

    gather[2].wait_sib()
    gather[2].finish_near()
    gather[2].finish_far()
    for h in range(2):
        up[:, cols[h]] = nn(proj[...], r["grads"][:, cols[h]])
        cell(1, h)
        sums[1][h].start(back(1, h))
    acc[...] = tn(proj[...], top[...])
    sums[1][0].mid()
    proj_sum.start(lambda dest: acc[pl.ds(pl.multiple_of(dest * c, c), c), :])
    sums[1][1].mid()
    high_term(1)
    proj_sum.mid()
    add_up(1, 0)
    cell(0, 0)
    sums[1][0].drain()
    sums[0][0].start(back(0, 0))
    proj_sum.finish()
    r["encoded"][...] = (
        proj_sum.own[...] + proj_sum.lin[...].astype(F32) + proj_sum.rin[...].astype(F32)
        + column(jnp.concatenate([r["pbias"][...], jnp.zeros((1, 128 - c), F32)], axis=1))[:c]).astype(BF)
    owner_pick(r["asked2"], r["encoded"], r["pick_out"])
    picked.start()
    d_high[1].mid()
    add_up(1, 1)
    cell(0, 1)
    sums[1][1].drain()
    high_term(0)
    sums[0][0].mid()
    sums[0][1].start(back(0, 1))
    d_high[1].turn()
    sums[0][1].mid()
    d_high[0].mid()
    d_high[1].mid2()
    picked.wait()
    token_pick(r["slot"], r["pick_in"], r["tok"])
    store = pltpu.make_async_copy(r["tok"], r["tokens"], r["raw_s"].at[3])
    store.start()
    r["dp_out"][...] = nt(r["grads"][...], top[...]).astype(BF)
    d_proj.start()
    d_high[0].turn()
    high_sum(1)
    d_high[0].mid2()
    add_up(0, 0)
    add_up(0, 1)
    r["d_features"][...] = up[...].T.astype(BF)
    d_proj.wait()
    got = jnp.zeros((proj_rows, filters), F32)
    for i in range(n_dp):
        got = got + r["dp_in"][i * proj_rows:(i + 1) * proj_rows, :].astype(F32)
    r["d_proj"][...] = got
    high_sum(0)
    store.wait()
    for x in (asked, slots, picked, d_proj, d_high[0], d_high[1], gather[2], *sums[0], proj_sum):
        x.drain()


def step(features, weight, bias, proj, pbias, slot, d_tokens, requests, n_dp):
    filters, words = features.shape
    total = weight.shape[1]
    c, tokens = d_tokens.shape
    width = proj.shape[1]
    cap = requests.shape[1]
    bufs = {
        "whole0": ((total, words), BF), "whole1": ((total, words), BF), "grads": ((width, words), BF),
        "top": ((filters, words), BF), "acc": ((2 * filters, words), F32),
        "bcol": ((2 * filters, 128), F32),
        "t": ((2, filters, words), F32), "g": ((2, filters, words), F32),
        "pre": ((2, 2 * filters, words), BF), "up": ((filters, words), F32),
        "sacc": ((n_dp * c, cap), F32),
        "slot_out": ((n_dp * c, cap), BF), "slot_in": ((n_dp * c, cap), BF),
        "pick_out": ((n_dp * c, cap), BF), "pick_in": ((n_dp * c, cap), BF),
        "row": ((c, words), BF), "encoded": ((c, words), BF),
        "dp_out": ((width, filters), BF), "dp_in": ((width, filters), BF),
        "dt": ((c, tokens), BF), "tok": ((c, tokens), BF),
        "weight": ((2, total, 2 * filters), BF), "raw": ((total, 2, filters), BF),
        "wanted": ((n_dp, 1, cap), jnp.int32), "asked": ((n_dp, 1, cap), jnp.int32), "asked2": ((n_dp, cap), jnp.int32),
    }
    for l in range(2):
        side = math.isqrt(n_dp)
        bufs[f"dh{l}_out"] = ((side, side, total // n_dp, 2 * filters), BF)
        for j, spec in enumerate(plane_bufs(side, total // n_dp, filters)):
            bufs[f"dh{l}_{j}"] = spec
    for l in range(2):
        for h in range(2):
            for j, spec in enumerate(scatter_bufs(filters, words // 2)):
                if l != 1 or j not in (0, 2):
                    bufs[f"rs{l}{h}_{j}"] = spec
    for j, spec in enumerate(scatter_bufs(c, words)):
        bufs[f"rs2_{j}"] = spec
    scratch = [pltpu.VMEM(*spec) for spec in bufs.values()]
    sems = {"ag": (3, 13), "rs": (5, 10), "dp": (4, n_dp), "ring": (8, 6), "raw": (4,)}
    names = tuple(bufs)
    for name, dims in sems.items():
        names += (name + "_s", name + "_r")
        scratch += [pltpu.SemaphoreType.DMA(dims)] * 2
    return pl.pallas_call(
        functools.partial(step_kernel, names),
        in_specs=[pl.BlockSpec(memory_space=pl.ANY) if x in ("weight_in", "d_tokens") else VM for x in INPUTS], out_specs=[pl.BlockSpec(memory_space=pl.ANY) if x == "tokens" else VM for x in OUTPUTS],
        out_shape=[
            jax.ShapeDtypeStruct((c, tokens), BF),
            jax.ShapeDtypeStruct((words, filters), BF),
            jax.ShapeDtypeStruct((2, total // n_dp, 2, filters), F32),
            jax.ShapeDtypeStruct((width // n_dp, filters), F32),
        ],
        scratch_shapes=scratch,
        compiler_params=pltpu.CompilerParams(
            collective_id=0, has_side_effects=True, vmem_limit_bytes=62 << 20),
    )(features, weight, bias, proj, pbias, slot, d_tokens, requests)


def hand_on(*arrays):
    n = len(arrays)

    def kernel(*refs):
        for i in range(n):
            refs[n + i][...] = refs[i][...]

    return pl.pallas_call(
        kernel, in_specs=[VM] * n, out_specs=[VM] * n,
        out_shape=[jax.ShapeDtypeStruct(a.shape, a.dtype) for a in arrays],
        compiler_params=pltpu.CompilerParams(vmem_limit_bytes=63 << 20),
    )(*arrays)


def per_device(chars, char_table, conv_weight, conv_bias, hw_weight, hw_bias, proj_weight,
               proj_bias, owner_types, requests, tok_slot, d_tokens):
    taps, embed_width, filters = conv_weight.shape
    layers, total = hw_weight.shape[:2]
    unique = owner_types.shape[0]
    owners, cap = requests.shape[1:]
    tokens, c = d_tokens.shape
    features = encode(chars.T, owner_types.reshape(1, unique), char_table.T,
                      conv_weight.reshape(taps * embed_width, filters),
                      conv_bias.reshape(1, filters), total)
    outs = step(
        features, hw_weight, hw_bias, proj_weight, proj_bias.reshape(1, c),
        tok_slot.reshape(1, tokens), d_tokens.T, requests.reshape(owners, cap), owners)
    tok, d_feat, d_high, d_proj = hand_on(*outs)
    return tok.T, d_feat, d_high, d_proj.T


def solution(mesh):
    return jax.shard_map(
        per_device,
        mesh=mesh,
        in_specs=(
            P("dp", None), P(), P(None, None, "enc"), P("enc"), P(None, None, None, "enc"),
            P(None, None, "enc"), P("enc", None), P("enc"), P("dp"), P("dp", None, None),
            P("dp"), P("dp", "enc"),
        ),
        out_specs=(P("dp", "enc"), P("dp", "enc"), P(None, "dp", None, "enc"), P("enc", "dp")),
        check_vma=False,
    )
```
